256 devices in a mesh: lat: 64 (over y, z, core), lev: 4 (over x).
Axes of the slice: x: 4, y: 4, z: 8, core: 2. Of those that a mesh axis runs over, the one named last changes fastest.
Arguments:
- fourier: bfloat16 [1280, 2, 64, 2, 640], P('lat', None, 'lev'), may hold values from -6 to 6
- quadrature: float32 [1280], P('lat'), may hold values from 0.3 to 3
- counts: int32 [1280], replicated, may hold values from 4 to 2576, as said below
- folded: int32 [640], replicated, may hold values from 0 to 639, as said below
- basis: bfloat16 [640, 640, 640], P('lat'), may hold values from -0.25 to 0.25
- vertical: bfloat16 [64, 64], P('lev'), may hold values from -0.75 to 0.75
- damping: float32 [640], replicated, may hold values from 0.2 to 1
Outputs:
- spectral: bfloat16 [640, 2, 64, 2, 640], P('lat', None, 'lev')
- grid: bfloat16 [1280, 2, 64, 2, 640], P('lat', None, 'lev')
The draws below stay inside these ranges and needn't reach their ends.
Inputs may be any that keep to these rules, and one draw needn't show every extreme that they name: `counts`: each count is a multiple of 4 and at most 20 + 4 min(j, 1279 - j) for latitude j; the two equatorial latitudes reach that bound and the two polar ones hold 4 points. folded is a permutation of the wavenumbers; slots d * 10 to (d + 1) * 10 - 1 belong to index d of lat, and the wavenumbers of every such block have the same sum.
All inputs are finite; a program needn't handle non-finite values.
Results may differ from the reference program's by a relative error of at most 0.0069.
Values may be sent and summed in bfloat16 or wider, within the bound.
No kernel may reach another device: no remote copies, remote signals or barrier semaphores. Data moves between devices by JAX's collectives and lax.ppermute only.
A program may use at most 128 MiB of HBM per device.

```python
import math
import jax
import jax.numpy as jnp
from jax import lax

NLAT = 1280
TRUNC = 640
FIELDS = 2
LEVELS = 64
HALF = 640
MDEV = 10


def draw_counts(key, part):
    key = jax.random.fold_in(key, 11)
    rows = jnp.arange(NLAT, dtype=jnp.int32)
    distance = jnp.minimum(rows, NLAT - 1 - rows)
    shaved = jax.random.randint(key, (NLAT,), 0, 5)
    shaved = jnp.where(distance == 0, 4, jnp.where(distance == NLAT // 2 - 1, 0, shaved))
    return (20 + 4 * distance - 4 * shaved).astype(jnp.int32)


def draw_folded(key, part):
    key = jax.random.fold_in(key, 23)
    first_key, second_key = jax.random.split(key)
    owners = TRUNC // MDEV
    pair_count = MDEV // 2
    device_ids = jnp.arange(owners, dtype=jnp.int32)[:, None]
    rounds = jnp.arange(pair_count, dtype=jnp.int32)[None, :]
    lower = 2 * owners * rounds + device_ids
    upper = 2 * owners * (rounds + 1) - 1 - device_ids
    blocks = jnp.concatenate([lower, upper], axis=1)
    blocks = blocks[jax.random.permutation(first_key, owners)]
    inner_keys = jax.random.split(second_key, owners)
    shuffles = jax.vmap(lambda inner: jax.random.permutation(inner, MDEV))(inner_keys)
    blocks = jnp.take_along_axis(blocks, shuffles, axis=1)
    return blocks.reshape(TRUNC).astype(jnp.int32)


def steps_of(own_key, extent, shards, low, high):
    factor_of, own = 1.0, jax.random.fold_in(own_key, 6)
    for axis_at, parts in shards:
        steps = jnp.exp(jax.random.uniform(jax.random.fold_in(own, axis_at), (parts,), jnp.float32, low / len(shards), high / len(shards)))
        factor_of = factor_of * jnp.repeat(steps, extent[axis_at] // parts).reshape([-1 if axis == axis_at else 1 for axis in range(len(extent))])
    return factor_of


def gaussian(own_key, shape, deviation, reach, pieces=(), held_as=jnp.bfloat16):
    array = deviation * jax.random.normal(own_key, shape, jnp.float32)
    if pieces:
        array = array * steps_of(own_key, shape, pieces, -0.22, 0.18)
    return jnp.clip(array, -reach, reach).astype(held_as)


def setup_inputs(seed: int = 0) -> dict:
    key_of = jax.random.split(jax.random.key(seed), 8)
    return {
        "fourier": gaussian(key_of[0], (NLAT, FIELDS, LEVELS, 2, TRUNC), 1.0, 6.0, ((0, 64), (2, 4))),
        "quadrature": jnp.clip(jnp.exp(math.log(3.0) - 2.3025851 * jax.random.uniform(key_of[1], (NLAT,), jnp.float32) ** steps_of(key_of[1], (NLAT,), ((0, 64),), -0.2, 0.2)), 0.3, 3.0),
        "counts": draw_counts(jax.random.fold_in(key_of[7], 71), 0),
        "folded": draw_folded(jax.random.fold_in(key_of[7], 71), 0),
        "basis": gaussian(key_of[4], (TRUNC, HALF, TRUNC), HALF ** -0.5, 0.25, ((0, 64),)),
        "vertical": gaussian(key_of[5], (LEVELS, LEVELS), LEVELS ** -0.5, 0.75, ((0, 4),)),
        "damping": jnp.clip(jnp.exp(jax.random.uniform(key_of[6], (TRUNC,), jnp.float32, math.log(0.2), math.log(1.0))), 0.2, 1.0),
    }


def reference(fourier, quadrature, counts, folded, basis, vertical, damping):
    batch = FIELDS * LEVELS * 2
    orders = jnp.arange(TRUNC, dtype=jnp.int32)
    resolved = (2 * orders[None, :] < counts[:, None])[:, None, None, None, :]
    weighted = jnp.where(resolved, fourier.astype(jnp.float32) * quadrature[:, None, None, None, None], 0.0).astype(jnp.bfloat16)
    columns = jnp.moveaxis(jnp.take(weighted.reshape(NLAT, batch, TRUNC), folded, axis=2), 2, 0)
    vertical_f = vertical.astype(jnp.float32)

    def one_slot(inputs):
        column, table, wave = inputs
        northern = column[:HALF].astype(jnp.float32)
        southern = column[HALF:][::-1].astype(jnp.float32)
        symmetric = (northern + southern).astype(jnp.bfloat16)
        antisym = (northern - southern).astype(jnp.bfloat16)
        matching = (orders + wave) % 2 == 0
        from_sym = jnp.dot(symmetric.T, table, preferred_element_type=jnp.float32)
        from_anti = jnp.dot(antisym.T, table, preferred_element_type=jnp.float32)
        spectra = jnp.where(matching[None, :], from_sym, from_anti)
        spectra = jnp.where(orders[None, :] >= wave, spectra, 0.0).astype(jnp.bfloat16)
        shaped = spectra.reshape(FIELDS, LEVELS, 2, TRUNC).astype(jnp.float32)
        mixed = jnp.einsum("lq,fqcn->flcn", vertical_f, shaped)
        filtered = (mixed * damping).astype(jnp.bfloat16).reshape(batch, TRUNC)
        kept = jnp.where(matching[None, :], filtered, jnp.zeros_like(filtered))
        flipped = jnp.where(matching[None, :], jnp.zeros_like(filtered), filtered)
        even_part = jnp.dot(table, kept.T, preferred_element_type=jnp.float32)
        odd_part = jnp.dot(table, flipped.T, preferred_element_type=jnp.float32)
        north_out = (even_part + odd_part).astype(jnp.bfloat16)
        south_out = (even_part - odd_part).astype(jnp.bfloat16)[::-1]
        return spectra, jnp.concatenate([north_out, south_out], axis=0)

    spectra_all, grid_slots = lax.map(one_slot, (columns, basis, folded))
    spectral = spectra_all.reshape(TRUNC, FIELDS, LEVELS, 2, TRUNC)
    inverse = jnp.zeros((TRUNC,), jnp.int32).at[folded].set(orders)
    regrid = jnp.moveaxis(jnp.take(grid_slots, inverse, axis=0), 0, 2).reshape(NLAT, FIELDS, LEVELS, 2, TRUNC)
    grid = jnp.where(resolved, regrid, jnp.zeros_like(regrid))
    return spectral, grid
```

```python
import numpy as np
import jax
import jax.numpy as jnp
from jax import lax
from jax.experimental import pallas as pl
from jax.experimental.pallas import tpu as pltpu
from jax.sharding import PartitionSpec as P

F32, BF16 = jnp.float32, jnp.bfloat16
AXES = ("lat", "lev")
OWN = 64
LEV = 4
ROWS = 20
SLOTS = 10
LOCAL = 16
WAVES = 640
HALF = 640
QUADS = 5
CHUNK = 26
STRIDE = LEV * CHUNK
TOTAL = OWN * STRIDE
VMEM = 60 * 1024 * 1024


def row_order():
    a, f, l, c = np.meshgrid(np.arange(4), np.arange(2), np.arange(LOCAL), np.arange(2), indexing="ij")
    source = ((a * 2 + f) * LOCAL + l) * 2 + c
    target = ((f * 2 + c) * 4 + a) * LOCAL + l
    out = np.zeros((256, 256), np.float32)
    out[target.ravel(), source.ravel()] = 1
    return out


def lane_orders():
    h, x, k, a, l = np.meshgrid(np.arange(2), np.arange(LEV), np.arange(2), np.arange(4), np.arange(LOCAL), indexing="ij")
    source = (((h * LEV + x) * 2 + k) * 4 + a) * LOCAL + l
    place = np.where(h == 0, a, 3 - a)
    there = np.zeros((1024, 1024), np.float32)
    back = np.zeros((1024, 1024), np.float32)
    for q in range(2):
        target = (((place * 2 + k) * 2 + q) * LEV + x) * LOCAL + l
        there[source.ravel(), target.ravel()] = np.where((h == 1) & (q == 1), -1, 1).ravel()
        same = h == q
        back[target[same], source[same]] = 1
    return there, back


def one_hot(folded_ref, hot):
    lanes = lax.broadcasted_iota(jnp.int32, (OWN, WAVES), 1)
    for k in range(SLOTS):
        hot[k * OWN : (k + 1) * OWN, :] = jnp.where(folded_ref[:, k : k + 1] == lanes, 1.0, 0.0).astype(BF16)


def low_lanes(rows):
    return lax.broadcasted_iota(jnp.int32, (rows, 128), 1) < 64


def outward(place, counts, quad, fourier, folded, order, out, hot, weighted, stage):
    quarter = pl.program_id(0)

    @pl.when(quarter == 0)
    def _():
        one_hot(folded, hot)
        stage[pl.ds(CHUNK - 1, OWN * LEV, stride=CHUNK), :] = jnp.zeros((OWN * LEV, 128), F32)

    lanes = 2 * lax.broadcasted_iota(jnp.int32, (64, WAVES), 1)
    for a in range(4):
        row = quarter * 4 + a
        count = counts[place[0] * ROWS + row]
        product = fourier[a].astype(F32) * quad[row]
        weighted[a * 64 : (a + 1) * 64, :] = jnp.where(lanes < count, product, 0.0).astype(BF16)
    ordered = jnp.dot(order[...], weighted[...], preferred_element_type=F32).astype(BF16)
    low = low_lanes(OWN)
    for pair in range(QUADS):
        both = lax.dot_general(
            hot[pair * 128 : (pair + 1) * 128, :], ordered, (((1,), (1,)), ((), ())), preferred_element_type=F32
        )
        first, second = both[:OWN], both[OWN:]
        for half in range(2):
            left, right = first[:, half * 128 : (half + 1) * 128], second[:, half * 128 : (half + 1) * 128]
            start = pair * QUADS + quarter
            stage[pl.ds(2 * half * CHUNK + start, OWN, stride=STRIDE), :] = jnp.where(
                low, left, pltpu.roll(right, 64, 1)
            )
            stage[pl.ds((2 * half + 1) * CHUNK + start, OWN, stride=STRIDE), :] = jnp.where(
                low, pltpu.roll(left, 64, 1), right
            )

    @pl.when(quarter == QUADS - 1)
    def _():
        out[...] = stage[...].astype(BF16)


def middle(waves, received, basis, there, back, vertical, damping, spectral, out, stage, mixed_up, columns, turn):
    slot = pl.program_id(0)
    half = OWN // 2
    group = QUADS * half

    @pl.when(slot == 0)
    def _():
        turn[...] = jnp.where(
            lax.broadcasted_iota(jnp.int32, (group, group), 0) + lax.broadcasted_iota(jnp.int32, (group, group), 1)
            == group - 1,
            1.0,
            0.0,
        ).astype(BF16)
        stage[...] = received[...].astype(F32)
        for pair in range(QUADS):
            for quarter in range(QUADS):
                rows = slice(pair * group + quarter * half, pair * group + (quarter + 1) * half)
                for side in range(2):
                    for x in range(LEV):
                        lanes = slice((side * LEV + x) * 128, (side * LEV + x + 1) * 128)
                        start = (side * half * LEV + x) * CHUNK + pair * QUADS + quarter
                        mixed_up[rows, lanes] = stage[pl.ds(start, half, stride=STRIDE), :].astype(BF16)
            rows = slice(pair * group, (pair + 1) * group)
            mixed_up[rows, 512:] = jnp.dot(turn[...], mixed_up[rows, 512:], preferred_element_type=F32).astype(BF16)
        for pair in range(QUADS):
            rows = slice(pair * group, (pair + 1) * group)
            sums = jnp.dot(mixed_up[rows, :], there[...], preferred_element_type=F32)
            for quarter in range(QUADS):
                for a in range(4):
                    for k in range(2):
                        columns[2 * pair + k, pl.ds(quarter * 4 + a, half, stride=ROWS), :] = sums[
                            quarter * half : (quarter + 1) * half, (a * 2 + k) * 128 : (a * 2 + k + 1) * 128
                        ]

    wave = waves[slot]
    table = basis[0]
    both = columns[slot].T.astype(BF16)
    products = jnp.dot(both, table, preferred_element_type=F32)
    degrees = lax.broadcasted_iota(jnp.int32, (64, WAVES), 1)
    matching = (degrees + wave) % 2 == 0
    spectra = jnp.where(matching, products[:64], products[64:])
    spectra = jnp.where(degrees >= wave, spectra, 0.0).astype(BF16)
    for x in range(LEV):
        spectral[x, 0] = spectra[x * LOCAL : (x + 1) * LOCAL]
    filtered = jnp.dot(vertical[...], spectra, preferred_element_type=F32) * damping[...]
    signed = jnp.where(matching, filtered, -filtered)
    stacked = jnp.concatenate([filtered, signed], axis=0).astype(BF16)
    columns[slot] = lax.dot_general(table, stacked, (((1,), (1,)), ((), ())), preferred_element_type=F32)

    @pl.when(slot == SLOTS - 1)
    def _():
        stage[pl.ds(CHUNK - 1, OWN * LEV, stride=CHUNK), :] = jnp.zeros((OWN * LEV, 128), F32)
        for pair in range(QUADS):
            for quarter in range(QUADS):
                rows = slice(pair * group + quarter * half, pair * group + (quarter + 1) * half)
                for a in range(4):
                    for k in range(2):
                        mixed_up[rows, (a * 2 + k) * 128 : (a * 2 + k + 1) * 128] = columns[
                            2 * pair + k, pl.ds(quarter * 4 + a, half, stride=ROWS), :
                        ].astype(BF16)
        for pair in range(QUADS):
            rows = slice(pair * group, (pair + 1) * group)
            moved = jnp.dot(mixed_up[rows, :], back[...], preferred_element_type=F32)
            south = jnp.dot(turn[...], moved[:, 512:].astype(BF16), preferred_element_type=F32)
            for quarter in range(QUADS):
                part = slice(quarter * half, (quarter + 1) * half)
                for x in range(LEV):
                    start = x * CHUNK + pair * QUADS + quarter
                    lanes = slice(x * 128, (x + 1) * 128)
                    stage[pl.ds(start, half, stride=STRIDE), :] = moved[part, lanes]
                    stage[pl.ds(half * STRIDE + start, half, stride=STRIDE), :] = south[part, lanes]
        out[...] = stage[...].astype(BF16)


def homeward(place, counts, received, folded, order, grid, hot, slots, stage):
    quarter = pl.program_id(0)

    @pl.when(quarter == 0)
    def _():
        one_hot(folded, hot)
        stage[...] = received[...].astype(F32)

    low = low_lanes(OWN)
    for pair in range(QUADS):
        for half in range(2):
            start = pair * QUADS + quarter
            left = stage[pl.ds(2 * half * CHUNK + start, OWN, stride=STRIDE), :]
            right = stage[pl.ds((2 * half + 1) * CHUNK + start, OWN, stride=STRIDE), :]
            lanes = slice(half * 128, (half + 1) * 128)
            slots[(2 * pair) * OWN : (2 * pair + 1) * OWN, lanes] = jnp.where(
                low, left, pltpu.roll(right, 64, 1)
            ).astype(BF16)
            slots[(2 * pair + 1) * OWN : (2 * pair + 2) * OWN, lanes] = jnp.where(
                low, pltpu.roll(left, 64, 1), right
            ).astype(BF16)
    turned = lax.dot_general(
        order[...], slots[...], (((1,), (1,)), ((), ())), preferred_element_type=F32
    ).astype(BF16)
    values = jnp.dot(turned, hot[...], preferred_element_type=F32)
    lanes = 2 * lax.broadcasted_iota(jnp.int32, (64, WAVES), 1)
    for a in range(4):
        count = counts[place[0] * ROWS + quarter * 4 + a]
        grid[a] = jnp.where(lanes < count, values[a * 64 : (a + 1) * 64], 0.0).astype(BF16)


def smem():
    return pl.BlockSpec(memory_space=pltpu.SMEM)


def fixed(shape):
    return pl.BlockSpec(shape, lambda i: (0,) * len(shape))


def exchange(blocks):
    blocks = blocks.reshape(TOTAL // 2, 2, 128).reshape(OWN * LEV, CHUNK // 2, 2, 128)
    blocks = lax.all_to_all(blocks, AXES, split_axis=0, concat_axis=0, tiled=True)
    return blocks.reshape(TOTAL // 2, 2, 128).reshape(TOTAL, 128)


def on_device(fourier, quadrature, counts, folded, basis, vertical, damping):
    place = lax.axis_index("lat").astype(jnp.int32)
    params = pltpu.CompilerParams(vmem_limit_bytes=VMEM, dimension_semantics=("arbitrary",))
    whole_vertical = lax.all_gather(vertical, "lev", axis=0, tiled=True)
    owners = folded.reshape(OWN, SLOTS)
    my_waves = lax.dynamic_slice_in_dim(folded, place * SLOTS, SLOTS)
    order = row_order()
    there, back = lane_orders()
    place = place[None]

    sent = pl.pallas_call(
        outward,
        grid=(QUADS,),
        in_specs=[
            smem(),
            smem(),
            smem(),
            pl.BlockSpec((4, 64, WAVES), lambda i: (i, 0, 0)),
            fixed((OWN, SLOTS)),
            fixed((256, 256)),
        ],
        out_specs=fixed((TOTAL, 128)),
        out_shape=jax.ShapeDtypeStruct((TOTAL, 128), BF16),
        scratch_shapes=[
            pltpu.VMEM((WAVES, WAVES), BF16),
            pltpu.VMEM((256, WAVES), BF16),
            pltpu.VMEM((TOTAL, 128), F32),
        ],
        compiler_params=params,
    )(place, counts, quadrature, fourier.reshape(ROWS, 64, WAVES), owners, jnp.asarray(order, BF16))

    received = exchange(sent)

    spectral, sent = pl.pallas_call(
        middle,
        grid=(SLOTS,),
        in_specs=[
            smem(),
            fixed((TOTAL, 128)),
            pl.BlockSpec((1, HALF, WAVES), lambda i: (i, 0, 0)),
            fixed((1024, 1024)),
            fixed((1024, 1024)),
            fixed((64, 64)),
            fixed((1, WAVES)),
        ],
        out_specs=[pl.BlockSpec((LEV, 1, LOCAL, WAVES), lambda i: (0, i, 0, 0)), fixed((TOTAL, 128))],
        out_shape=[
            jax.ShapeDtypeStruct((LEV, SLOTS, LOCAL, WAVES), BF16),
            jax.ShapeDtypeStruct((TOTAL, 128), BF16),
        ],
        scratch_shapes=[
            pltpu.VMEM((TOTAL, 128), F32),
            pltpu.VMEM((800, 1024), BF16),
            pltpu.VMEM((SLOTS, HALF, 128), F32),
            pltpu.VMEM((160, 160), BF16),
        ],
        compiler_params=params,
    )(
        my_waves,
        received,
        basis,
        jnp.asarray(there, BF16),
        jnp.asarray(back, BF16),
        whole_vertical,
        damping.reshape(1, WAVES),
    )

    received = exchange(sent)
    parts = lax.all_to_all(spectral, "lev", split_axis=0, concat_axis=0, tiled=True)
    parts = parts.reshape(2, 2, SLOTS, LOCAL, WAVES).transpose(2, 0, 3, 1, 4)

    grid = pl.pallas_call(
        homeward,
        grid=(QUADS,),
        in_specs=[smem(), smem(), fixed((TOTAL, 128)), fixed((OWN, SLOTS)), fixed((256, 256))],
        out_specs=pl.BlockSpec((4, 64, WAVES), lambda i: (i, 0, 0)),
        out_shape=jax.ShapeDtypeStruct((ROWS, 64, WAVES), BF16),
        scratch_shapes=[
            pltpu.VMEM((WAVES, WAVES), BF16),
            pltpu.VMEM((WAVES, 256), BF16),
            pltpu.VMEM((TOTAL, 128), F32),
        ],
        compiler_params=params,
    )(place, counts, received, owners, jnp.asarray(order.T, BF16))
    return parts, grid.reshape(ROWS, 2, LOCAL, 2, WAVES)


def solution(mesh):
    return jax.shard_map(
        on_device,
        mesh=mesh,
        in_specs=(
            P("lat", None, "lev", None, None),
            P("lat"),
            P(),
            P(),
            P("lat", None, None),
            P("lev", None),
            P(),
        ),
        out_specs=(P("lat", None, "lev", None, None), P("lat", None, "lev", None, None)),
        check_vma=False,
    )
```

```python
import numpy as np
import jax
import jax.numpy as jnp
from jax import lax
from jax.experimental import pallas as pl
from jax.experimental.pallas import tpu as pltpu
from jax.sharding import PartitionSpec as P

F32, BF16 = jnp.float32, jnp.bfloat16
AXES = ("lat", "lev")
OWN = 64
HEMI = 32
LEV = 4
ROWS = 20
SLOTS = 10
LOCAL = 16
WAVES = 640
HALF = 640
QUADS = 5
GROUP = QUADS * HEMI
CHUNK = 26
STRIDE = LEV * CHUNK
TOTAL = OWN * STRIDE
VMEM = 28 * 1024 * 1024
ORDER = [d if d < HEMI else OWN - 1 + HEMI - d for d in range(OWN)]
GROUPS = [[d * LEV + x for d in ORDER for x in range(LEV)]]


def lane_order():
    x, k, a, l = np.meshgrid(np.arange(LEV), np.arange(2), np.arange(4), np.arange(LOCAL), indexing="ij")
    out = np.zeros((512, 512), np.float32)
    out[(((x * 2 + k) * 4 + a) * LOCAL + l).ravel(), (((a * 2 + k) * LEV + x) * LOCAL + l).ravel()] = 1
    return out


def low_lanes(rows):
    return lax.broadcasted_iota(jnp.int32, (rows, 128), 1) < 64


def nt(left, right):
    return lax.dot_general(left, right, (((1,), (1,)), ((), ())), preferred_element_type=F32)


def one_hot(folded, column, hot):
    row = folded[...].astype(F32).reshape(1, WAVES)
    for t in range(WAVES // 128):
        lanes = slice(t * 128, (t + 1) * 128)
        column[lanes, :] = jnp.broadcast_to(row[:, lanes], (128, 128)).T
    i = lax.broadcasted_iota(jnp.int32, (OWN, OWN), 0)
    d = lax.broadcasted_iota(jnp.int32, (OWN, OWN), 1)
    turn = jnp.where(d == jnp.where(i < HEMI, i, OWN - 1 + HEMI - i), 1.0, 0.0).astype(BF16)
    lanes = lax.broadcasted_iota(jnp.int32, (OWN, 128), 1)
    for k in range(SLOTS):
        waves = column[pl.ds(k, OWN, stride=SLOTS), :].astype(jnp.int32)
        plain = jnp.concatenate(
            [jnp.where(waves == lanes + t * 128, 1.0, 0.0).astype(BF16) for t in range(WAVES // 128)], axis=1
        )
        hot[k * OWN : (k + 1) * OWN, :] = jnp.dot(turn, plain, preferred_element_type=F32).astype(BF16)


def outward(place, counts, quad, fourier, folded, vertical, out, hot, weighted, stage, column, couple):
    quarter = pl.program_id(0)
    south = place[0] >= HEMI
    where = jnp.where(south, QUADS - 1 - quarter, quarter)

    @pl.when(quarter == 0)
    def _():
        one_hot(folded, column, hot)
        couple[...] = vertical[...].astype(F32)
        piece = 2 * lax.rem(place[0], 8)
        line = jnp.concatenate([couple[pl.ds(piece, 1), :], couple[pl.ds(piece + 1, 1), :]], axis=1)
        stage[pl.ds(CHUNK - 1, OWN * LEV, stride=CHUNK), :] = jnp.broadcast_to(line, (OWN * LEV, 128))

    lanes = 2 * lax.broadcasted_iota(jnp.int32, (LEV * LOCAL, WAVES), 1)
    for a in range(4):
        row = quarter * 4 + a
        count = counts[place[0] * ROWS + row]
        product = fourier[a].astype(F32) * quad[row]
        product = jnp.where(lanes < count, product, 0.0).astype(BF16)
        at = jnp.where(south, 3 - a, a)
        for x in range(LEV):
            weighted[pl.ds(pl.multiple_of((x * 4 + at) * LOCAL, LOCAL), LOCAL), :] = product[
                x * LOCAL : (x + 1) * LOCAL
            ]
    low = low_lanes(OWN)
    for pair in range(QUADS):
        both = nt(hot[pair * 128 : (pair + 1) * 128, :], weighted[...])
        first, second = both[:OWN], both[OWN:]
        for half in range(2):
            left, right = first[:, half * 128 : (half + 1) * 128], second[:, half * 128 : (half + 1) * 128]
            start = pair * QUADS + where
            stage[pl.ds(2 * half * CHUNK + start, OWN, stride=STRIDE), :] = jnp.where(
                low, left, pltpu.roll(right, 64, 1)
            )
            stage[pl.ds((2 * half + 1) * CHUNK + start, OWN, stride=STRIDE), :] = jnp.where(
                low, pltpu.roll(left, 64, 1), right
            )

    @pl.when(quarter == QUADS - 1)
    def _():
        out[...] = stage[...].astype(BF16)


def middle(
    place, folded, received, basis, order, damping, own, first, second, third, out, stage, sums, columns, turned, couple
):
    slot = pl.program_id(0)
    pair = slot // 2

    @pl.when(slot == 0)
    def _():
        stage[...] = received[...].astype(F32)
        for x in range(LEV):
            lines = stage[pl.ds(x * CHUNK + CHUNK - 1, 8, stride=STRIDE), :]
            couple[pl.ds(x * LOCAL, 8, stride=2), :] = lines
            couple[pl.ds(x * LOCAL + 1, 8, stride=2), :] = pltpu.roll(lines, 64, 1)

    @pl.when(slot % 2 == 0)
    def _():
        for quarter in range(QUADS):
            rows = slice(quarter * HEMI, (quarter + 1) * HEMI)
            for x in range(LEV):
                start = x * CHUNK + pair * QUADS + quarter
                lanes = slice(x * 128, (x + 1) * 128)
                north = stage[pl.ds(start, HEMI, stride=STRIDE), :]
                south = stage[pl.ds(HEMI * STRIDE + start, HEMI, stride=STRIDE), :]
                sums[0, rows, lanes] = (north + south).astype(BF16)
                sums[1, rows, lanes] = (north - south).astype(BF16)
        for side in range(2):
            placed = jnp.dot(sums[side], order[...], preferred_element_type=F32)
            for quarter in range(QUADS):
                for a in range(4):
                    columns[side, pl.ds(quarter * 4 + a, HEMI, stride=ROWS), :] = placed[
                        quarter * HEMI : (quarter + 1) * HEMI, a * 128 : (a + 1) * 128
                    ]
            across = columns[side].T.astype(BF16)
            for k in range(2):
                turned[k, side * 64 : (side + 1) * 64, :] = across[k * 64 : (k + 1) * 64]

    wave = folded[place[0] * SLOTS + slot]
    table = basis[0]
    odd = slot % 2
    products = jnp.dot(turned[odd], table, preferred_element_type=F32)
    degrees = lax.broadcasted_iota(jnp.int32, (64, WAVES), 1)
    matching = (degrees + wave) % 2 == 0
    spectra = jnp.where(matching, products[:64], products[64:])
    spectra = jnp.where(degrees >= wave, spectra, 0.0).astype(BF16)
    for x in range(LEV):
        piece = spectra[x * LOCAL : (x + 1) * LOCAL]
        ahead = lax.rem(x - place[1] + LEV, LEV)
        for o, ref in enumerate((own, first, second, third)):

            @pl.when(ahead == o)
            def _():
                ref[0] = piece

    filtered = jnp.dot(couple[:, :64].astype(BF16), spectra, preferred_element_type=F32) * damping[...].reshape(1, WAVES)
    signed = jnp.where(matching, filtered, -filtered)
    stacked = jnp.concatenate([filtered, signed], axis=0).astype(BF16)
    columns[odd] = nt(table, stacked)

    @pl.when(odd == 1)
    def _():
        low = low_lanes(HEMI)
        for quarter in range(QUADS):
            rows = slice(quarter * HEMI, (quarter + 1) * HEMI)
            for a in range(4):
                lanes = slice(a * 128, (a + 1) * 128)
                left = columns[0, pl.ds(quarter * 4 + a, HEMI, stride=ROWS), :]
                right = columns[1, pl.ds(quarter * 4 + a, HEMI, stride=ROWS), :]
                sums[0, rows, lanes] = jnp.where(low, left, pltpu.roll(right, 64, 1)).astype(BF16)
                sums[1, rows, lanes] = jnp.where(low, pltpu.roll(left, 64, 1), right).astype(BF16)
        for side in range(2):
            placed = nt(sums[side], order[...])
            for quarter in range(QUADS):
                for x in range(LEV):
                    start = (side * HEMI * LEV + x) * CHUNK + pair * QUADS + quarter
                    stage[pl.ds(start, HEMI, stride=STRIDE), :] = placed[
                        quarter * HEMI : (quarter + 1) * HEMI, x * 128 : (x + 1) * 128
                    ]

    @pl.when(slot == SLOTS - 1)
    def _():
        out[...] = stage[...].astype(BF16)


def homeward(place, counts, received, hot, grid, slots, stage):
    quarter = pl.program_id(0)
    south = place[0] >= HEMI
    where = jnp.where(south, QUADS - 1 - quarter, quarter)

    @pl.when(quarter == 0)
    def _():
        stage[...] = received[...].astype(F32)

    low = low_lanes(OWN)
    for pair in range(QUADS):
        for half in range(2):
            start = pair * QUADS + where
            left = stage[pl.ds(2 * half * CHUNK + start, OWN, stride=STRIDE), :]
            right = stage[pl.ds((2 * half + 1) * CHUNK + start, OWN, stride=STRIDE), :]
            lanes = slice(half * 128, (half + 1) * 128)
            slots[(2 * pair) * OWN : (2 * pair + 1) * OWN, lanes] = jnp.where(
                low, left, pltpu.roll(right, 64, 1)
            ).astype(BF16)
            slots[(2 * pair + 1) * OWN : (2 * pair + 2) * OWN, lanes] = jnp.where(
                low, pltpu.roll(left, 64, 1), right
            ).astype(BF16)
    values = jnp.dot(slots[...].T, hot[...], preferred_element_type=F32)
    lanes = 2 * lax.broadcasted_iota(jnp.int32, (LOCAL, WAVES), 1)
    for at in range(4):
        a = jnp.where(south, 3 - at, at)
        count = counts[place[0] * ROWS + quarter * 4 + a]
        for x in range(LEV):
            rows = slice((x * 4 + at) * LOCAL, (x * 4 + at + 1) * LOCAL)
            grid[a, x * LOCAL : (x + 1) * LOCAL, :] = jnp.where(lanes < count, values[rows], 0.0).astype(BF16)


def smem():
    return pl.BlockSpec(memory_space=pltpu.SMEM)


def fixed(*shape):
    return pl.BlockSpec(shape, lambda i: (0,) * len(shape))


def params(limit=VMEM):
    return pltpu.CompilerParams(vmem_limit_bytes=limit, dimension_semantics=("arbitrary",))


def call_outward(place, counts, quadrature, fourier, folded, vertical):
    return pl.pallas_call(
        outward,
        grid=(QUADS,),
        in_specs=[
            smem(),
            smem(),
            smem(),
            pl.BlockSpec((4, 64, WAVES), lambda i: (i, 0, 0)),
            fixed(WAVES),
            fixed(LOCAL, LEV * LOCAL),
        ],
        out_specs=[fixed(TOTAL, 128), fixed(WAVES, WAVES)],
        out_shape=[jax.ShapeDtypeStruct((TOTAL, 128), BF16), jax.ShapeDtypeStruct((WAVES, WAVES), BF16)],
        scratch_shapes=[
            pltpu.VMEM((256, WAVES), BF16),
            pltpu.VMEM((TOTAL, 128), F32),
            pltpu.VMEM((WAVES, 128), F32),
            pltpu.VMEM((LOCAL, LEV * LOCAL), F32),
        ],
        compiler_params=params(),
    )(place, counts, quadrature, fourier, folded, vertical)


def call_middle(place, folded, received, basis, damping):
    piece = pl.BlockSpec((1, LOCAL, WAVES), lambda i: (i, 0, 0))
    return pl.pallas_call(
        middle,
        grid=(SLOTS,),
        in_specs=[
            smem(),
            smem(),
            fixed(TOTAL, 128),
            pl.BlockSpec((1, HALF, WAVES), lambda i: (i, 0, 0)),
            fixed(512, 512),
            fixed(WAVES),
        ],
        out_specs=[piece] * LEV + [fixed(TOTAL, 128)],
        out_shape=[jax.ShapeDtypeStruct((SLOTS, LOCAL, WAVES), BF16)] * LEV
        + [jax.ShapeDtypeStruct((TOTAL, 128), BF16)],
        scratch_shapes=[
            pltpu.VMEM((TOTAL, 128), F32),
            pltpu.VMEM((2, GROUP, 512), BF16),
            pltpu.VMEM((2, HALF, 128), F32),
            pltpu.VMEM((2, 128, HALF), BF16),
            pltpu.VMEM((64, 128), F32),
        ],
        compiler_params=params(),
    )(place, folded, received, basis, jnp.asarray(lane_order(), BF16), damping)


def call_homeward(place, counts, received, hot):
    return pl.pallas_call(
        homeward,
        grid=(QUADS,),
        in_specs=[smem(), smem(), fixed(TOTAL, 128), fixed(WAVES, WAVES)],
        out_specs=pl.BlockSpec((4, 64, WAVES), lambda i: (i, 0, 0)),
        out_shape=jax.ShapeDtypeStruct((ROWS, 64, WAVES), BF16),
        scratch_shapes=[
            pltpu.VMEM((WAVES, 256), BF16),
            pltpu.VMEM((TOTAL, 128), F32),
        ],
        compiler_params=params(),
    )(place, counts, received, hot)


def exchange(blocks):
    blocks = blocks.reshape(TOTAL // 2, 2, 128).reshape(OWN * LEV, CHUNK // 2, 2, 128)
    blocks = lax.all_to_all(blocks, AXES, split_axis=0, concat_axis=0, tiled=True, axis_index_groups=GROUPS)
    return blocks.reshape(TOTAL // 2, 2, 128).reshape(TOTAL, 128)


def on_device(fourier, quadrature, counts, folded, basis, vertical, damping):
    lev = lax.axis_index("lev").astype(jnp.int32)
    place = jnp.stack([lax.axis_index("lat").astype(jnp.int32), lev])
    fourier = fourier.transpose(0, 1, 3, 2, 4).reshape(ROWS, 64, WAVES)
    sent, hot = call_outward(place, counts, quadrature, fourier, folded, vertical)
    *pieces, sent = call_middle(place, folded, exchange(sent), basis, damping)
    parts = pieces[:1] + [
        lax.ppermute(pieces[o], "lev", [(i, (i + o) % LEV) for i in range(LEV)]) for o in range(1, LEV)
    ]
    received = exchange(sent)
    parts = jnp.stack(parts)
    parts = jnp.stack([lax.dynamic_index_in_dim(parts, (lev - x) % LEV, 0, keepdims=False) for x in range(LEV)])
    spectral = parts.reshape(2, 2, SLOTS, LOCAL, WAVES).transpose(2, 0, 3, 1, 4)
    grid = call_homeward(place, counts, received, hot)
    return spectral, grid.reshape(ROWS, 2, 2, LOCAL, WAVES).transpose(0, 1, 3, 2, 4)


def solution(mesh):
    return jax.shard_map(
        on_device,
        mesh=mesh,
        in_specs=(
            P("lat", None, "lev", None, None),
            P("lat"),
            P(),
            P(),
            P("lat", None, None),
            P("lev", None),
            P(),
        ),
        out_specs=(P("lat", None, "lev", None, None), P("lat", None, "lev", None, None)),
        check_vma=False,
    )
```

```python
import numpy as np
import jax
import jax.numpy as jnp
from jax import lax
from jax.experimental import pallas as pl
from jax.experimental.pallas import tpu as pltpu
from jax.sharding import PartitionSpec as P

F32, BF16 = jnp.float32, jnp.bfloat16
AXES = ("lat", "lev")
OWN = 64
HEMI = 32
LEV = 4
ROWS = 20
SLOTS = 10
LOCAL = 16
WAVES = 640
HALF = 640
QUADS = 5
GROUP = QUADS * HEMI
CHUNK = 26
STRIDE = LEV * CHUNK
TOTAL = OWN * STRIDE
VMEM = 24 * 1024 * 1024
UNROLL = True
ORDER = [d if d < HEMI else OWN - 1 + HEMI - d for d in range(OWN)]
GROUPS = [[d * LEV + x for d in ORDER for x in range(LEV)]]


def lane_order():
    x, a, k, l = np.meshgrid(np.arange(LEV), np.arange(4), np.arange(2), np.arange(LOCAL), indexing="ij")
    out = np.zeros((512, 512), np.float32)
    out[(((x * 4 + a) * 2 + k) * LOCAL + l).ravel(), (((a * LEV + x) * 2 + k) * LOCAL + l).ravel()] = 1
    return out


def row_order():
    t, j = np.meshgrid(np.arange(HEMI), np.arange(ROWS), indexing="ij")
    out = np.zeros((HALF, HALF), np.float32)
    out[(j * HEMI + t).ravel(), (t * ROWS + j).ravel()] = 1
    return out


def low_lanes(rows):
    return lax.broadcasted_iota(jnp.int32, (rows, 128), 1) < 64


def one_hot(folded, column, hot):
    row = folded[...].astype(F32).reshape(1, WAVES)
    for t in range(WAVES // 128):
        lanes = slice(t * 128, (t + 1) * 128)
        column[lanes, :] = jnp.broadcast_to(row[:, lanes], (128, 128)).T
    i = lax.broadcasted_iota(jnp.int32, (OWN, OWN), 0)
    d = lax.broadcasted_iota(jnp.int32, (OWN, OWN), 1)
    turn = jnp.where(d == jnp.where(i < HEMI, i, OWN - 1 + HEMI - i), 1.0, 0.0).astype(BF16)
    lanes = lax.broadcasted_iota(jnp.int32, (OWN, 128), 1)
    for k in range(SLOTS):
        waves = column[pl.ds(k, OWN, stride=SLOTS), :].astype(jnp.int32)
        plain = jnp.concatenate(
            [jnp.where(waves == lanes + t * 128, 1.0, 0.0).astype(BF16) for t in range(WAVES // 128)], axis=1
        )
        hot[k * OWN : (k + 1) * OWN, :] = jnp.dot(turn, plain, preferred_element_type=F32).astype(BF16)


def swap_halves(low, left, right):
    return jnp.where(low, left, pltpu.roll(right, 64, 1)), jnp.where(low, pltpu.roll(left, 64, 1), right)


def outward(place, counts, quad, fourier, folded, vertical, out, hot, weighted, stage, column, couple):
    south = place[0] >= HEMI
    one_hot(folded, column, hot)
    couple[...] = vertical[...].astype(F32)
    piece = 2 * lax.rem(place[0], 8)
    line = jnp.concatenate([couple[pl.ds(piece, 1), :], couple[pl.ds(piece + 1, 1), :]], axis=1)
    stage[pl.ds(CHUNK - 1, OWN * LEV, stride=CHUNK), :] = jnp.broadcast_to(line, (OWN * LEV, 128))
    lanes = 2 * lax.broadcasted_iota(jnp.int32, (LEV * LOCAL, WAVES), 1)
    low = low_lanes(LOCAL)
    slotted = hot[...].T

    @pl.loop(0, QUADS, unroll=UNROLL)
    def _(quarter):
        where = jnp.where(south, QUADS - 1 - quarter, quarter)
        for a in range(4):
            row = quarter * 4 + a
            count = counts[place[0] * ROWS + row]
            product = fourier[row].astype(F32) * quad[row]
            product = jnp.where(lanes < count, product, 0.0).astype(BF16)
            at = jnp.where(south, 3 - a, a)
            for x in range(LEV):
                weighted[quarter, pl.ds(pl.multiple_of((x * 4 + at) * LOCAL, LOCAL), LOCAL), :] = product[
                    x * LOCAL : (x + 1) * LOCAL
                ]
        spread = jnp.dot(weighted[quarter], slotted, preferred_element_type=F32)

        def part(x, a, tile):
            return spread[(x * 4 + a) * LOCAL : (x * 4 + a + 1) * LOCAL, tile * 128 : (tile + 1) * 128]

        def put(x, row, values):
            stage[pl.ds(x * CHUNK + row, OWN, stride=STRIDE), :] = values

        for x in range(LEV):
            for a in (0, 2):
                blocks = [block for tile in range(4) for block in swap_halves(low, part(x, a, tile), part(x, a + 1, tile))]
                across = jnp.concatenate(blocks, axis=0).T
                put(x, where * 4 + a, across[:OWN])
                put(x, where * 4 + a + 1, across[OWN:])
        for x in (0, 2):
            blocks = [block for a in range(4) for block in swap_halves(low, part(x, a, 4), part(x + 1, a, 4))]
            across = jnp.concatenate(blocks, axis=0).T
            put(x, ROWS + where, across[:OWN])
            put(x + 1, ROWS + where, across[OWN:])

    out[...] = stage[...].astype(BF16)


def prepare(basis, order, table, across):
    rows = jnp.dot(order[...], basis[0], preferred_element_type=F32)
    table[0] = rows.astype(BF16)
    across[0] = rows.T.astype(BF16)


def middle(
    place, folded, received, table, across, order, back, damping,
    own, first, second, third, out, stage, turned, couple, pieces, result, rest,
):
    stage[...] = received[...].astype(F32)
    for x in range(LEV):
        lines = stage[pl.ds(x * CHUNK + CHUNK - 1, 8, stride=STRIDE), :]
        couple[pl.ds(x * LOCAL, 8, stride=2), :] = lines
        couple[pl.ds(x * LOCAL + 1, 8, stride=2), :] = pltpu.roll(lines, 64, 1)
    mixing = couple[:, :64].astype(BF16)
    damp = damping[...].reshape(1, WAVES)
    degrees = lax.broadcasted_iota(jnp.int32, (64, WAVES), 1)

    def both(x, row):
        north = stage[pl.ds(x * CHUNK + row, HEMI, stride=STRIDE), :]
        south = stage[pl.ds((HEMI * LEV + x) * CHUNK + row, HEMI, stride=STRIDE), :]
        return north + south, north - south

    def split(side, x, k, values):
        turned[k, (side * LEV + x) * LOCAL : (side * LEV + x + 1) * LOCAL, :] = values.astype(BF16)

    for quarter in range(QUADS):
        rows = slice(quarter * HEMI, (quarter + 1) * HEMI)
        for x in range(LEV):
            for side, values in enumerate(both(x, ROWS + quarter)):
                rest[side * GROUP + quarter * HEMI : side * GROUP + (quarter + 1) * HEMI, x * 128 : (x + 1) * 128] = (
                    values.astype(BF16)
                )
    placed = jnp.dot(rest[...], order[...], preferred_element_type=F32)
    for side in range(2):
        values = jnp.concatenate(
            [
                placed[side * GROUP + quarter * HEMI : side * GROUP + (quarter + 1) * HEMI, a * 128 : (a + 1) * 128]
                for quarter in range(QUADS)
                for a in range(4)
            ],
            axis=0,
        ).T
        for x in range(LEV):
            for k in range(2):
                split(side, x, 8 + k, values[(x * 2 + k) * LOCAL : (x * 2 + k + 1) * LOCAL])
    for x in range(LEV):
        pairs = [both(x, row) for row in range(ROWS)]
        for side in range(2):
            values = jnp.concatenate([pair[side] for pair in pairs], axis=0).T
            for k in range(8):
                split(side, x, k, values[k * LOCAL : (k + 1) * LOCAL])

    def one_slot(slot):
        wave = folded[place[0] * SLOTS + slot]
        products = jnp.dot(turned[slot], table[slot], preferred_element_type=F32)
        matching = ((degrees ^ wave) & 1) == 0
        spectra = jnp.where(matching, products[:64], products[64:])
        spectra = jnp.where(degrees >= wave, spectra, 0.0).astype(BF16)
        pieces[slot] = spectra
        for o, ref in enumerate((own, first, second, third)):
            ahead = pl.multiple_of(lax.rem(place[1] + o, LEV) * LOCAL, LOCAL)
            ref[slot] = pieces[slot, pl.ds(ahead, LOCAL), :]
        filtered = jnp.dot(mixing, spectra, preferred_element_type=F32) * damp
        signed = jnp.where(matching, filtered, -filtered)
        stacked = jnp.concatenate([filtered, signed], axis=0).astype(BF16)
        values = jnp.dot(stacked, across[slot], preferred_element_type=F32)
        return [values[block * LOCAL : (block + 1) * LOCAL] for block in range(2 * LEV)]

    for slot in range(8):
        for block, values in enumerate(one_slot(slot)):
            result[block, slot * LOCAL : (slot + 1) * LOCAL, :] = values
    for slot in range(8, SLOTS):
        for block, values in enumerate(one_slot(slot)):
            side, x = divmod(block, LEV)
            at = (x * 2 + slot - 8) * LOCAL
            result[2 * LEV + side, at : at + LOCAL, :] = values

    for side in range(2):
        values = result[2 * LEV + side].T.astype(BF16)
        for quarter in range(QUADS):
            for a in range(4):
                row = quarter * 4 + a
                rest[side * GROUP + quarter * HEMI : side * GROUP + (quarter + 1) * HEMI, a * 128 : (a + 1) * 128] = (
                    values[row * HEMI : (row + 1) * HEMI]
                )
    placed = jnp.dot(rest[...], back[...], preferred_element_type=F32)
    for block in range(2 * LEV):
        side, x = divmod(block, LEV)
        values = result[block].T
        start = block * CHUNK if side == 0 else (HEMI * LEV + x) * CHUNK
        for row in range(ROWS):
            stage[pl.ds(start + row, HEMI, stride=STRIDE), :] = values[row * HEMI : (row + 1) * HEMI]
        for quarter in range(QUADS):
            stage[pl.ds(start + ROWS + quarter, HEMI, stride=STRIDE), :] = placed[
                side * GROUP + quarter * HEMI : side * GROUP + (quarter + 1) * HEMI, x * 128 : (x + 1) * 128
            ]
    out[...] = stage[...].astype(BF16)


def homeward(place, counts, received, hot, grid, slots, stage):
    south = place[0] >= HEMI
    stage[...] = received[...].astype(F32)
    low = low_lanes(LOCAL)
    lanes = 2 * lax.broadcasted_iota(jnp.int32, (LOCAL, WAVES), 1)

    @pl.loop(0, QUADS, unroll=UNROLL)
    def _(quarter):
        where = jnp.where(south, QUADS - 1 - quarter, quarter)

        def get(x, row):
            return stage[pl.ds(x * CHUNK + row, OWN, stride=STRIDE), :]

        def put(x, a, tile, values):
            slots[quarter, (x * 4 + a) * LOCAL : (x * 4 + a + 1) * LOCAL, tile * 128 : (tile + 1) * 128] = values.astype(BF16)

        for x in range(LEV):
            for a in (0, 2):
                values = jnp.concatenate([get(x, where * 4 + a), get(x, where * 4 + a + 1)], axis=0).T
                for tile in range(4):
                    even = values[2 * tile * LOCAL : (2 * tile + 1) * LOCAL]
                    odd = values[(2 * tile + 1) * LOCAL : (2 * tile + 2) * LOCAL]
                    left, right = swap_halves(low, even, odd)
                    put(x, a, tile, left)
                    put(x, a + 1, tile, right)
        for x in (0, 2):
            values = jnp.concatenate([get(x, ROWS + where), get(x + 1, ROWS + where)], axis=0).T
            for a in range(4):
                even = values[2 * a * LOCAL : (2 * a + 1) * LOCAL]
                odd = values[(2 * a + 1) * LOCAL : (2 * a + 2) * LOCAL]
                left, right = swap_halves(low, even, odd)
                put(x, a, 4, left)
                put(x + 1, a, 4, right)
        values = jnp.dot(slots[quarter], hot[...], preferred_element_type=F32)
        for at in range(4):
            row = quarter * 4 + jnp.where(south, 3 - at, at)
            count = counts[place[0] * ROWS + row]
            for x in range(LEV):
                part = values[(x * 4 + at) * LOCAL : (x * 4 + at + 1) * LOCAL]
                grid[row, x * LOCAL : (x + 1) * LOCAL, :] = jnp.where(lanes < count, part, 0.0).astype(BF16)


def smem():
    return pl.BlockSpec(memory_space=pltpu.SMEM)


def in_vmem():
    return pl.BlockSpec(memory_space=pltpu.VMEM)


def call(kernel, scalars, arrays, outs, scratch):
    outs = [jax.ShapeDtypeStruct(shape, BF16) for shape in outs]
    return pl.pallas_call(
        kernel,
        in_specs=[smem() for _ in scalars] + [in_vmem() for _ in arrays],
        out_specs=[in_vmem() for _ in outs],
        out_shape=outs,
        scratch_shapes=[pltpu.VMEM(shape, dtype) for shape, dtype in scratch],
        compiler_params=pltpu.CompilerParams(vmem_limit_bytes=VMEM),
    )(*scalars, *arrays)


def call_outward(place, counts, quadrature, fourier, folded, vertical):
    return call(
        outward,
        (place, counts, quadrature),
        (fourier, folded, vertical),
        [(TOTAL, 128), (WAVES, WAVES)],
        [((QUADS, 256, WAVES), BF16), ((TOTAL, 128), F32), ((WAVES, 128), F32), ((LOCAL, LEV * LOCAL), F32)],
    )


def call_prepare(basis):
    block = pl.BlockSpec((1, HALF, WAVES), lambda i: (i, 0, 0))
    shape = jax.ShapeDtypeStruct((SLOTS, HALF, WAVES), BF16)
    return pl.pallas_call(
        prepare,
        grid=(SLOTS,),
        in_specs=[block, pl.BlockSpec((HALF, HALF), lambda i: (0, 0))],
        out_specs=[block, block],
        out_shape=[shape, shape],
        cost_estimate=pl.CostEstimate(flops=SLOTS * HALF**3 * 2, bytes_accessed=SLOTS * HALF**2 * 6, transcendentals=0),
        compiler_params=pltpu.CompilerParams(vmem_limit_bytes=16 * 1024 * 1024),
    )(basis, jnp.asarray(row_order(), BF16))


def call_middle(place, folded, received, tables, damping):
    order = lane_order()
    return call(
        middle,
        (place, folded),
        (received, *tables, jnp.asarray(order, BF16), jnp.asarray(order.T, BF16), damping),
        [(SLOTS, LOCAL, WAVES)] * LEV + [(TOTAL, 128)],
        [
            ((TOTAL, 128), F32),
            ((SLOTS, 128, HALF), BF16),
            ((64, 128), F32),
            ((SLOTS, 64, WAVES), BF16),
            ((2 * LEV + 2, 128, HALF), F32),
            ((2 * GROUP, 512), BF16),
        ],
    )


def call_homeward(place, counts, received, hot):
    (grid,) = call(
        homeward, (place, counts), (received, hot), [(ROWS, 64, WAVES)], [((QUADS, 256, WAVES), BF16), ((TOTAL, 128), F32)]
    )
    return grid


def exchange(blocks):
    blocks = blocks.reshape(TOTAL // 2, 2, 128).reshape(OWN * LEV, CHUNK // 2, 2, 128)
    blocks = lax.all_to_all(blocks, AXES, split_axis=0, concat_axis=0, tiled=True, axis_index_groups=GROUPS)
    return blocks.reshape(TOTAL // 2, 2, 128).reshape(TOTAL, 128)


def on_device(fourier, quadrature, counts, folded, basis, vertical, damping):
    lev = lax.axis_index("lev").astype(jnp.int32)
    place = jnp.stack([lax.axis_index("lat").astype(jnp.int32), lev])
    fourier = fourier.transpose(0, 1, 3, 2, 4).reshape(ROWS, 64, WAVES)
    sent, hot = call_outward(place, counts, quadrature, fourier, folded, vertical)
    *pieces, sent = call_middle(place, folded, exchange(sent), call_prepare(basis), damping)
    parts = pieces[:1] + [
        lax.ppermute(pieces[o], "lev", [(i, (i + o) % LEV) for i in range(LEV)]) for o in range(1, LEV)
    ]
    received = exchange(sent)
    parts = jnp.stack(parts)
    parts = jnp.stack([lax.dynamic_index_in_dim(parts, (lev - x) % LEV, 0, keepdims=False) for x in range(LEV)])
    spectral = parts.reshape(2, 2, SLOTS, LOCAL, WAVES).transpose(2, 0, 3, 1, 4)
    grid = call_homeward(place, counts, received, hot)
    return spectral, grid.reshape(ROWS, 2, 2, LOCAL, WAVES).transpose(0, 1, 3, 2, 4)


def solution(mesh):
    return jax.shard_map(
        on_device,
        mesh=mesh,
        in_specs=(
            P("lat", None, "lev", None, None),
            P("lat"),
            P(),
            P(),
            P("lat", None, None),
            P("lev", None),
            P(),
        ),
        out_specs=(P("lat", None, "lev", None, None), P("lat", None, "lev", None, None)),
        check_vma=False,
    )
```

```python
import jax
import jax.numpy as jnp
from jax import lax
from jax.experimental import pallas as pl
from jax.experimental.pallas import tpu as pltpu
from jax.sharding import PartitionSpec as P

F32, BF16 = jnp.float32, jnp.bfloat16
AXES = ("lat", "lev")
OWN = 64
HEMI = 32
LEV = 4
ROWS = 20
SLOTS = 10
LOCAL = 16
WAVES = 640
HALF = 640
QUADS = 5
GROUP = QUADS * HEMI
CHUNK = 26
STRIDE = LEV * CHUNK
TOTAL = OWN * STRIDE
VMEM = 24 * 1024 * 1024
UNROLL = True
ORDER = [d if d < HEMI else OWN - 1 + HEMI - d for d in range(OWN)]
GROUPS = [[d * LEV + x for d in ORDER for x in range(LEV)]]


def low_lanes(rows):
    return lax.broadcasted_iota(jnp.int32, (rows, 128), 1) < 64


def one_hot(folded, column, hot):
    row = folded[...].astype(F32).reshape(1, WAVES)
    for t in range(WAVES // 128):
        lanes = slice(t * 128, (t + 1) * 128)
        column[lanes, :] = jnp.broadcast_to(row[:, lanes], (128, 128)).T
    i = lax.broadcasted_iota(jnp.int32, (OWN, OWN), 0)
    d = lax.broadcasted_iota(jnp.int32, (OWN, OWN), 1)
    turn = jnp.where(d == jnp.where(i < HEMI, i, OWN - 1 + HEMI - i), 1.0, 0.0).astype(BF16)
    lanes = lax.broadcasted_iota(jnp.int32, (OWN, 128), 1)
    for k in range(SLOTS):
        waves = column[pl.ds(k, OWN, stride=SLOTS), :].astype(jnp.int32)
        plain = jnp.concatenate(
            [jnp.where(waves == lanes + t * 128, 1.0, 0.0).astype(BF16) for t in range(WAVES // 128)], axis=1
        )
        hot[k * OWN : (k + 1) * OWN, :] = jnp.dot(turn, plain, preferred_element_type=F32).astype(BF16)


def swap_halves(low, left, right):
    return jnp.where(low, left, pltpu.roll(right, 64, 1)), jnp.where(low, pltpu.roll(left, 64, 1), right)


def outward(place, counts, quad, fourier, folded, vertical, out, hot, weighted, stage, column, couple):
    south = place[0] >= HEMI
    one_hot(folded, column, hot)
    couple[...] = vertical[...].astype(F32)
    piece = 2 * lax.rem(place[0], 8)
    line = jnp.concatenate([couple[pl.ds(piece, 1), :], couple[pl.ds(piece + 1, 1), :]], axis=1)
    stage[pl.ds(CHUNK - 1, OWN * LEV, stride=CHUNK), :] = jnp.broadcast_to(line, (OWN * LEV, 128))
    lanes = 2 * lax.broadcasted_iota(jnp.int32, (LEV * LOCAL, WAVES), 1)
    low = low_lanes(LOCAL)
    slotted = hot[...].T

    @pl.loop(0, QUADS, unroll=UNROLL)
    def _(quarter):
        where = jnp.where(south, QUADS - 1 - quarter, quarter)
        for a in range(4):
            row = quarter * 4 + a
            count = counts[place[0] * ROWS + row]
            product = fourier[row].astype(F32) * quad[row]
            product = jnp.where(lanes < count, product, 0.0).astype(BF16)
            at = jnp.where(south, 3 - a, a)
            for x in range(LEV):
                weighted[quarter, pl.ds(pl.multiple_of((x * 4 + at) * LOCAL, LOCAL), LOCAL), :] = product[
                    x * LOCAL : (x + 1) * LOCAL
                ]
        spread = jnp.dot(weighted[quarter], slotted, preferred_element_type=F32)

        def part(x, a, tile):
            return spread[(x * 4 + a) * LOCAL : (x * 4 + a + 1) * LOCAL, tile * 128 : (tile + 1) * 128]

        def put(x, row, values):
            stage[pl.ds(x * CHUNK + row, OWN, stride=STRIDE), :] = values

        for x in range(LEV):
            for a in (0, 2):
                blocks = [block for tile in range(4) for block in swap_halves(low, part(x, a, tile), part(x, a + 1, tile))]
                across = jnp.concatenate(blocks, axis=0).T
                put(x, where * 4 + a, across[:OWN])
                put(x, where * 4 + a + 1, across[OWN:])
        for x in (0, 2):
            blocks = [block for a in range(4) for block in swap_halves(low, part(x, a, 4), part(x + 1, a, 4))]
            across = jnp.concatenate(blocks, axis=0).T
            put(x, ROWS + where, across[:OWN])
            put(x + 1, ROWS + where, across[OWN:])

    out[...] = stage[...].astype(BF16)


def middle(
    place, folded, received, damping, table,
    own, first, second, third, out, stage, turned, couple, pieces, result, rest, order, natural, ready, leave, depart,
):
    stage[...] = received[...].astype(F32)
    for x in range(LEV):
        lines = stage[pl.ds(x * CHUNK + CHUNK - 1, 8, stride=STRIDE), :]
        couple[pl.ds(x * LOCAL, 8, stride=2), :] = lines
        couple[pl.ds(x * LOCAL + 1, 8, stride=2), :] = pltpu.roll(lines, 64, 1)
    mixing = couple[:, :64].astype(BF16)
    damp = damping[...].reshape(1, WAVES)
    degrees = lax.broadcasted_iota(jnp.int32, (64, WAVES), 1)
    lanes = lax.broadcasted_iota(jnp.int32, (512, 512), 1)
    swapped = ((lanes >> 7) << 5) | (((lanes >> 5) & 3) << 7) | (lanes & 31)
    order[...] = jnp.where(lax.broadcasted_iota(jnp.int32, (512, 512), 0) == swapped, 1.0, 0.0).astype(BF16)

    def both(x, row):
        north = stage[pl.ds(x * CHUNK + row, HEMI, stride=STRIDE), :]
        south = stage[pl.ds((HEMI * LEV + x) * CHUNK + row, HEMI, stride=STRIDE), :]
        return north + south, north - south

    def split(side, x, k, values):
        turned[k, (side * LEV + x) * LOCAL : (side * LEV + x + 1) * LOCAL, :] = values.astype(BF16)

    for quarter in range(QUADS):
        rows = slice(quarter * HEMI, (quarter + 1) * HEMI)
        for x in range(LEV):
            for side, values in enumerate(both(x, ROWS + quarter)):
                rest[side * GROUP + quarter * HEMI : side * GROUP + (quarter + 1) * HEMI, x * 128 : (x + 1) * 128] = (
                    values.astype(BF16)
                )
    placed = jnp.dot(rest[...], order[...], preferred_element_type=F32)
    for side in range(2):
        for quarter in range(QUADS):
            for a in range(4):
                natural[2 * LEV + side, pl.ds(quarter * 4 + a, HEMI, stride=ROWS), :] = placed[
                    side * GROUP + quarter * HEMI : side * GROUP + (quarter + 1) * HEMI, a * 128 : (a + 1) * 128
                ]
        values = natural[2 * LEV + side].T
        for x in range(LEV):
            for k in range(2):
                split(side, x, 8 + k, values[(x * 2 + k) * LOCAL : (x * 2 + k + 1) * LOCAL])
    for x in range(LEV):
        for row in range(ROWS):
            for side, values in enumerate(both(x, row)):
                natural[side * LEV + x, pl.ds(row, HEMI, stride=ROWS), :] = values
        for side in range(2):
            values = natural[side * LEV + x].T
            for k in range(8):
                split(side, x, k, values[k * LOCAL : (k + 1) * LOCAL])

    stores = []

    def one_slot(slot):
        wave = folded[place[0] * SLOTS + slot]
        products = jnp.dot(turned[slot], table[slot], preferred_element_type=F32)
        matching = ((degrees ^ wave) & 1) == 0
        spectra = jnp.where(matching, products[:64], products[64:])
        spectra = jnp.where(degrees >= wave, spectra, 0.0).astype(BF16)
        pieces[slot] = spectra
        for o, ref in enumerate((own, first, second, third)):
            ahead = pl.multiple_of(lax.rem(place[1] + o, LEV) * LOCAL, LOCAL)
            store = pltpu.make_async_copy(pieces.at[slot, pl.ds(ahead, LOCAL), :], ref.at[slot], leave.at[slot, o])
            store.start()
            stores.append(store)
        filtered = jnp.dot(mixing, spectra, preferred_element_type=F32) * damp
        signed = jnp.where(matching, filtered, -filtered)
        stacked = jnp.concatenate([filtered, signed], axis=0).astype(BF16)
        values = lax.dot_general(stacked, table[slot], (((1,), (1,)), ((), ())), preferred_element_type=F32)
        return [values[block * LOCAL : (block + 1) * LOCAL] for block in range(2 * LEV)]

    for slot in range(8):
        for block, values in enumerate(one_slot(slot)):
            result[block, slot * LOCAL : (slot + 1) * LOCAL, :] = values
    for slot in range(8, SLOTS):
        for block, values in enumerate(one_slot(slot)):
            side, x = divmod(block, LEV)
            at = (x * 2 + slot - 8) * LOCAL
            result[2 * LEV + side, at : at + LOCAL, :] = values

    for side in range(2):
        natural[2 * LEV + side] = result[2 * LEV + side].T
        for quarter in range(QUADS):
            for a in range(4):
                rest[side * GROUP + quarter * HEMI : side * GROUP + (quarter + 1) * HEMI, a * 128 : (a + 1) * 128] = (
                    natural[2 * LEV + side, pl.ds(quarter * 4 + a, HEMI, stride=ROWS), :].astype(BF16)
                )
    placed = jnp.dot(rest[...], order[...], preferred_element_type=F32)
    for side in range(2):
        for x in range(LEV):
            natural[side * LEV + x] = result[side * LEV + x].T
            start = (side * HEMI * LEV + x) * CHUNK
            for row in range(ROWS):
                stage[pl.ds(start + row, HEMI, stride=STRIDE), :] = natural[
                    side * LEV + x, pl.ds(row, HEMI, stride=ROWS), :
                ]
            for quarter in range(QUADS):
                stage[pl.ds(start + ROWS + quarter, HEMI, stride=STRIDE), :] = placed[
                    side * GROUP + quarter * HEMI : side * GROUP + (quarter + 1) * HEMI, x * 128 : (x + 1) * 128
                ]
        rows = pl.ds(side * HEMI * STRIDE, HEMI * STRIDE)
        ready[rows, :] = stage[rows, :].astype(BF16)
        store = pltpu.make_async_copy(ready.at[rows, :], out.at[rows, :], depart.at[side])
        store.start()
        stores.append(store)
    for store in stores:
        store.wait()


def homeward(place, counts, received, hot, grid, slots, stage):
    south = place[0] >= HEMI
    stage[...] = received[...].astype(F32)
    low = low_lanes(LOCAL)
    lanes = 2 * lax.broadcasted_iota(jnp.int32, (LOCAL, WAVES), 1)

    @pl.loop(0, QUADS, unroll=UNROLL)
    def _(quarter):
        where = jnp.where(south, QUADS - 1 - quarter, quarter)

        def get(x, row):
            return stage[pl.ds(x * CHUNK + row, OWN, stride=STRIDE), :]

        def put(x, a, tile, values):
            slots[quarter, (x * 4 + a) * LOCAL : (x * 4 + a + 1) * LOCAL, tile * 128 : (tile + 1) * 128] = values.astype(BF16)

        for x in range(LEV):
            for a in (0, 2):
                values = jnp.concatenate([get(x, where * 4 + a), get(x, where * 4 + a + 1)], axis=0).T
                for tile in range(4):
                    even = values[2 * tile * LOCAL : (2 * tile + 1) * LOCAL]
                    odd = values[(2 * tile + 1) * LOCAL : (2 * tile + 2) * LOCAL]
                    left, right = swap_halves(low, even, odd)
                    put(x, a, tile, left)
                    put(x, a + 1, tile, right)
        for x in (0, 2):
            values = jnp.concatenate([get(x, ROWS + where), get(x + 1, ROWS + where)], axis=0).T
            for a in range(4):
                even = values[2 * a * LOCAL : (2 * a + 1) * LOCAL]
                odd = values[(2 * a + 1) * LOCAL : (2 * a + 2) * LOCAL]
                left, right = swap_halves(low, even, odd)
                put(x, a, 4, left)
                put(x + 1, a, 4, right)
        values = jnp.dot(slots[quarter], hot[...], preferred_element_type=F32)
        for at in range(4):
            row = quarter * 4 + jnp.where(south, 3 - at, at)
            count = counts[place[0] * ROWS + row]
            for x in range(LEV):
                part = values[(x * 4 + at) * LOCAL : (x * 4 + at + 1) * LOCAL]
                grid[row, x * LOCAL : (x + 1) * LOCAL, :] = jnp.where(lanes < count, part, 0.0).astype(BF16)


def smem():
    return pl.BlockSpec(memory_space=pltpu.SMEM)


def in_vmem():
    return pl.BlockSpec(memory_space=pltpu.VMEM)


def in_hbm():
    return pl.BlockSpec(memory_space=pltpu.HBM)


def call(kernel, scalars, arrays, outs, scratch, far_outs=(), limit=VMEM):
    shapes = [jax.ShapeDtypeStruct(shape, BF16) for shape in (*far_outs, *outs)]
    return pl.pallas_call(
        kernel,
        in_specs=[smem() for _ in scalars] + [in_vmem() for _ in arrays],
        out_specs=[in_hbm() for _ in far_outs] + [in_vmem() for _ in outs],
        out_shape=shapes,
        scratch_shapes=[
            kind(shape, dtype) if dtype is not None else kind(shape)
            for kind, shape, dtype in ((pltpu.VMEM, *s) if len(s) == 2 else s for s in scratch)
        ],
        compiler_params=pltpu.CompilerParams(vmem_limit_bytes=limit),
    )(*scalars, *arrays)


def copies(*shape):
    return (pltpu.SemaphoreType.DMA, shape, None)


def call_outward(place, counts, quadrature, fourier, folded, vertical):
    return call(
        outward,
        (place, counts, quadrature),
        (fourier, folded, vertical),
        [(TOTAL, 128), (WAVES, WAVES)],
        [((QUADS, 256, WAVES), BF16), ((TOTAL, 128), F32), ((WAVES, 128), F32), ((LOCAL, LEV * LOCAL), F32)],
    )


def call_middle(place, folded, received, table, damping):
    return call(
        middle,
        (place, folded),
        (received, damping, table),
        [],
        [
            ((TOTAL, 128), F32),
            ((SLOTS, 128, HALF), BF16),
            ((64, 128), F32),
            ((SLOTS, 64, WAVES), BF16),
            ((2 * LEV + 2, 128, HALF), F32),
            ((2 * GROUP, 512), BF16),
            ((512, 512), BF16),
            ((2 * LEV + 2, HALF, 128), F32),
            ((TOTAL, 128), BF16),
            copies(SLOTS, LEV),
            copies(2),
        ],
        far_outs=[(SLOTS, LOCAL, WAVES)] * LEV + [(TOTAL, 128)],
        limit=28 * 1024 * 1024,
    )


def call_homeward(place, counts, received, hot):
    (grid,) = call(
        homeward,
        (place, counts),
        (received, hot),
        [(ROWS, 64, WAVES)],
        [((QUADS, 256, WAVES), BF16), ((TOTAL, 128), F32)],
    )
    return grid


def exchange(blocks):
    blocks = blocks.reshape(TOTAL // 2, 2, 128).reshape(OWN * LEV, CHUNK // 2, 2, 128)
    blocks = lax.all_to_all(blocks, AXES, split_axis=0, concat_axis=0, tiled=True, axis_index_groups=GROUPS)
    return blocks.reshape(TOTAL // 2, 2, 128).reshape(TOTAL, 128)


def on_device(fourier, quadrature, counts, folded, basis, vertical, damping):
    lev = lax.axis_index("lev").astype(jnp.int32)
    place = jnp.stack([lax.axis_index("lat").astype(jnp.int32), lev])
    fourier = fourier.transpose(0, 1, 3, 2, 4).reshape(ROWS, 64, WAVES)
    sent, hot = call_outward(place, counts, quadrature, fourier, folded, vertical)
    *pieces, sent = call_middle(place, folded, exchange(sent), basis, damping)
    parts = pieces[:1] + [
        lax.ppermute(pieces[o], "lev", [(i, (i + o) % LEV) for i in range(LEV)]) for o in range(1, LEV)
    ]
    received = exchange(sent)
    parts = jnp.stack(parts)
    parts = jnp.stack([lax.dynamic_index_in_dim(parts, (lev - x) % LEV, 0, keepdims=False) for x in range(LEV)])
    spectral = parts.reshape(2, 2, SLOTS, LOCAL, WAVES).transpose(2, 0, 3, 1, 4)
    grid = call_homeward(place, counts, received, hot)
    return spectral, grid.reshape(ROWS, 2, 2, LOCAL, WAVES).transpose(0, 1, 3, 2, 4)


def solution(mesh):
    return jax.shard_map(
        on_device,
        mesh=mesh,
        in_specs=(
            P("lat", None, "lev", None, None),
            P("lat"),
            P(),
            P(),
            P("lat", None, None),
            P("lev", None),
            P(),
        ),
        out_specs=(P("lat", None, "lev", None, None), P("lat", None, "lev", None, None)),
        check_vma=False,
    )
```

```python
import jax
import jax.numpy as jnp
from jax import lax
from jax.experimental import pallas as pl
from jax.experimental.pallas import tpu as pltpu
from jax.sharding import PartitionSpec as P

F32, BF16 = jnp.float32, jnp.bfloat16
AXES = ("lat", "lev")
OWN = 64
HEMI = 32
LEV = 4
ROWS = 20
SLOTS = 10
LOCAL = 16
WAVES = 640
HALF = 640
TILES = WAVES // 128
QUADS = 5
GROUP = QUADS * HEMI
CHUNK = 26
STRIDE = LEV * CHUNK
TOTAL = OWN * STRIDE
VMEM = 24 * 1024 * 1024
UNROLL = True
ORDER = [d if d < HEMI else OWN - 1 + HEMI - d for d in range(OWN)]
GROUPS = [[d * LEV + x for d in ORDER for x in range(LEV)]]


def low_lanes(rows):
    return lax.broadcasted_iota(jnp.int32, (rows, 128), 1) < 64


def one_hot(folded, column, hot):
    row = folded[...].astype(F32).reshape(1, WAVES)
    for t in range(WAVES // 128):
        lanes = slice(t * 128, (t + 1) * 128)
        column[lanes, :] = jnp.broadcast_to(row[:, lanes], (128, 128)).T
    i = lax.broadcasted_iota(jnp.int32, (OWN, OWN), 0)
    d = lax.broadcasted_iota(jnp.int32, (OWN, OWN), 1)
    turn = jnp.where(d == jnp.where(i < HEMI, i, OWN - 1 + HEMI - i), 1.0, 0.0).astype(BF16)
    lanes = lax.broadcasted_iota(jnp.int32, (OWN, 128), 1)
    for k in range(SLOTS):
        waves = column[pl.ds(k, OWN, stride=SLOTS), :].astype(jnp.int32)
        plain = jnp.concatenate(
            [jnp.where(waves == lanes + t * 128, 1.0, 0.0).astype(BF16) for t in range(WAVES // 128)], axis=1
        )
        hot[k * OWN : (k + 1) * OWN, :] = jnp.dot(turn, plain, preferred_element_type=F32).astype(BF16)


def swap_halves(low, left, right):
    return jnp.where(low, left, pltpu.roll(right, 64, 1)), jnp.where(low, pltpu.roll(left, 64, 1), right)


def outward(place, counts, quad, fourier, folded, vertical, out, hot, weighted, stage, column, couple):
    south = place[0] >= HEMI
    one_hot(folded, column, hot)
    couple[...] = vertical[...].astype(F32)
    piece = 2 * lax.rem(place[0], 8)
    line = jnp.concatenate([couple[pl.ds(piece, 1), :], couple[pl.ds(piece + 1, 1), :]], axis=1)
    stage[pl.ds(CHUNK - 1, OWN * LEV, stride=CHUNK), :] = jnp.broadcast_to(line, (OWN * LEV, 128))
    lanes = 2 * lax.broadcasted_iota(jnp.int32, (LEV * LOCAL, WAVES), 1)
    low = low_lanes(LOCAL)
    slotted = hot[...].T

    @pl.loop(0, QUADS, unroll=UNROLL)
    def _(quarter):
        where = jnp.where(south, QUADS - 1 - quarter, quarter)
        for a in range(4):
            row = quarter * 4 + a
            count = counts[place[0] * ROWS + row]
            product = fourier[row].astype(F32) * quad[row]
            product = jnp.where(lanes < count, product, 0.0).astype(BF16)
            at = jnp.where(south, 3 - a, a)
            for x in range(LEV):
                weighted[quarter, pl.ds(pl.multiple_of((x * 4 + at) * LOCAL, LOCAL), LOCAL), :] = product[
                    x * LOCAL : (x + 1) * LOCAL
                ]
        spread = jnp.dot(weighted[quarter], slotted, preferred_element_type=F32)

        def part(x, a, tile):
            return spread[(x * 4 + a) * LOCAL : (x * 4 + a + 1) * LOCAL, tile * 128 : (tile + 1) * 128]

        def put(x, row, values):
            stage[pl.ds(x * CHUNK + row, OWN, stride=STRIDE), :] = values

        for x in range(LEV):
            for a in (0, 2):
                blocks = [block for tile in range(4) for block in swap_halves(low, part(x, a, tile), part(x, a + 1, tile))]
                across = jnp.concatenate(blocks, axis=0).T
                put(x, where * 4 + a, across[:OWN])
                put(x, where * 4 + a + 1, across[OWN:])
        for x in (0, 2):
            blocks = [block for a in range(4) for block in swap_halves(low, part(x, a, 4), part(x + 1, a, 4))]
            across = jnp.concatenate(blocks, axis=0).T
            put(x, ROWS + where, across[:OWN])
            put(x + 1, ROWS + where, across[OWN:])

    out[...] = stage[...].astype(BF16)


def middle(
    place, folded, received, damping, table,
    own, first, second, third, out, stage, turned, couple, pieces, result, rest, order, natural, ready, leave, depart,
):
    stage[...] = received[...].astype(F32)
    for x in range(LEV):
        lines = stage[pl.ds(x * CHUNK + CHUNK - 1, 8, stride=STRIDE), :]
        couple[pl.ds(x * LOCAL, 8, stride=2), :] = lines
        couple[pl.ds(x * LOCAL + 1, 8, stride=2), :] = pltpu.roll(lines, 64, 1)
    mixing = couple[:, :64].astype(BF16)
    damp = damping[...].reshape(1, WAVES)
    lanes = lax.broadcasted_iota(jnp.int32, (512, 512), 1)
    swapped = ((lanes >> 7) << 5) | (((lanes >> 5) & 3) << 7) | (lanes & 31)
    order[...] = jnp.where(lax.broadcasted_iota(jnp.int32, (512, 512), 0) == swapped, 1.0, 0.0).astype(BF16)

    def both(x, row):
        north = stage[pl.ds(x * CHUNK + row, HEMI, stride=STRIDE), :]
        south = stage[pl.ds((HEMI * LEV + x) * CHUNK + row, HEMI, stride=STRIDE), :]
        return north + south, north - south

    def split(side, x, k, values):
        turned[k, (side * LEV + x) * LOCAL : (side * LEV + x + 1) * LOCAL, :] = values.astype(BF16)

    for quarter in range(QUADS):
        rows = slice(quarter * HEMI, (quarter + 1) * HEMI)
        for x in range(LEV):
            for side, values in enumerate(both(x, ROWS + quarter)):
                rest[side * GROUP + quarter * HEMI : side * GROUP + (quarter + 1) * HEMI, x * 128 : (x + 1) * 128] = (
                    values.astype(BF16)
                )
    placed = jnp.dot(rest[...], order[...], preferred_element_type=F32)
    for side in range(2):
        for quarter in range(QUADS):
            for a in range(4):
                natural[2 * LEV + side, pl.ds(quarter * 4 + a, HEMI, stride=ROWS), :] = placed[
                    side * GROUP + quarter * HEMI : side * GROUP + (quarter + 1) * HEMI, a * 128 : (a + 1) * 128
                ]
        values = natural[2 * LEV + side].T
        for x in range(LEV):
            for k in range(2):
                split(side, x, 8 + k, values[(x * 2 + k) * LOCAL : (x * 2 + k + 1) * LOCAL])
    for x in range(LEV):
        for row in range(ROWS):
            for side, values in enumerate(both(x, row)):
                natural[side * LEV + x, pl.ds(row, HEMI, stride=ROWS), :] = values
        for side in range(2):
            values = natural[side * LEV + x].T
            for k in range(8):
                split(side, x, k, values[k * LOCAL : (k + 1) * LOCAL])

    degrees = lax.broadcasted_iota(jnp.int32, (64, WAVES), 1)

    def matching(slot):
        return ((degrees ^ folded[place[0] * SLOTS + slot]) & 1) == 0

    for slot in range(SLOTS):
        products = jnp.dot(turned[slot], table[slot], preferred_element_type=F32)
        spectra = jnp.where(matching(slot), products[:64], products[64:])
        spectra = jnp.where(degrees >= folded[place[0] * SLOTS + slot], spectra, 0.0)
        pieces[slot] = spectra.astype(BF16)
    stores = []
    for o, ref in enumerate((own, first, second, third)):
        ahead = pl.multiple_of(lax.rem(place[1] + o, LEV) * LOCAL, LOCAL)
        store = pltpu.make_async_copy(pieces.at[:, pl.ds(ahead, LOCAL), :], ref, leave.at[o])
        store.start()
        stores.append(store)

    for slot in range(SLOTS):
        filtered = jnp.dot(mixing, pieces[slot], preferred_element_type=F32) * damp
        signed = jnp.where(matching(slot), filtered, -filtered)
        turned[slot] = jnp.concatenate([filtered, signed], axis=0).astype(BF16)
    for slot in range(SLOTS):
        result[slot] = lax.dot_general(
            turned[slot], table[slot], (((1,), (1,)), ((), ())), preferred_element_type=F32
        )

    def gather(block, slots):
        return [result[slot, block * LOCAL : (block + 1) * LOCAL, :] for slot in slots]

    for side in range(2):
        natural[2 * LEV + side] = jnp.concatenate(
            [part for x in range(LEV) for part in gather(side * LEV + x, (8, 9))], axis=0
        ).T
        for quarter in range(QUADS):
            for a in range(4):
                rest[side * GROUP + quarter * HEMI : side * GROUP + (quarter + 1) * HEMI, a * 128 : (a + 1) * 128] = (
                    natural[2 * LEV + side, pl.ds(quarter * 4 + a, HEMI, stride=ROWS), :].astype(BF16)
                )
    placed = jnp.dot(rest[...], order[...], preferred_element_type=F32)
    for side in range(2):
        for x in range(LEV):
            natural[side * LEV + x] = jnp.concatenate(gather(side * LEV + x, range(8)), axis=0).T
            start = (side * HEMI * LEV + x) * CHUNK
            for row in range(ROWS):
                stage[pl.ds(start + row, HEMI, stride=STRIDE), :] = natural[
                    side * LEV + x, pl.ds(row, HEMI, stride=ROWS), :
                ]
            for quarter in range(QUADS):
                stage[pl.ds(start + ROWS + quarter, HEMI, stride=STRIDE), :] = placed[
                    side * GROUP + quarter * HEMI : side * GROUP + (quarter + 1) * HEMI, x * 128 : (x + 1) * 128
                ]
        for part in range(2):
            rows = pl.ds((2 * side + part) * (TOTAL // 4), TOTAL // 4)
            ready[rows, :] = stage[rows, :].astype(BF16)
            store = pltpu.make_async_copy(ready.at[rows, :], out.at[rows, :], depart.at[2 * side + part])
            store.start()
            stores.append(store)
    for store in stores:
        store.wait()


def homeward(place, counts, received, hot, out, grid, slots, stage, depart):
    stores = []
    south = place[0] >= HEMI
    stage[...] = received[...].astype(F32)
    low = low_lanes(LOCAL)
    lanes = 2 * lax.broadcasted_iota(jnp.int32, (LEV * LOCAL, WAVES), 1)

    def one_quarter(quarter):
        where = jnp.where(south, QUADS - 1 - quarter, quarter)

        def get(x, row):
            return stage[pl.ds(x * CHUNK + row, OWN, stride=STRIDE), :]

        def put(x, a, tile, values):
            f, c = divmod(x, 2)
            slots[quarter, tile, pl.ds(a * 64 + f * 32 + c, LOCAL, stride=2), :] = values

        for x in range(LEV):
            for a in (0, 2):
                values = jnp.concatenate([get(x, where * 4 + a), get(x, where * 4 + a + 1)], axis=0).T
                for tile in range(4):
                    even = values[2 * tile * LOCAL : (2 * tile + 1) * LOCAL]
                    odd = values[(2 * tile + 1) * LOCAL : (2 * tile + 2) * LOCAL]
                    left, right = swap_halves(low, even, odd)
                    put(x, a, tile, left)
                    put(x, a + 1, tile, right)
        for x in (0, 2):
            values = jnp.concatenate([get(x, ROWS + where), get(x + 1, ROWS + where)], axis=0).T
            for a in range(4):
                even = values[2 * a * LOCAL : (2 * a + 1) * LOCAL]
                odd = values[(2 * a + 1) * LOCAL : (2 * a + 2) * LOCAL]
                left, right = swap_halves(low, even, odd)
                put(x, a, 4, left)
                put(x + 1, a, 4, right)
        mixed = jnp.concatenate([slots[quarter, tile].astype(BF16) for tile in range(TILES)], axis=1)
        values = jnp.dot(mixed, hot[...], preferred_element_type=F32)
        for at in range(4):
            row = quarter * 4 + jnp.where(south, 3 - at, at)
            count = counts[place[0] * ROWS + row]
            part = jnp.where(lanes < count, values[at * 64 : (at + 1) * 64], 0.0).astype(BF16)
            grid[row] = part.reshape(2, LOCAL, 2, WAVES)
        rows = pl.ds(quarter * 4, 4)
        stores.append(pltpu.make_async_copy(grid.at[rows], out.at[rows], depart.at[quarter]))
        stores[-1].start()

    for quarter in range(QUADS):
        one_quarter(quarter)
    for store in stores:
        store.wait()


def smem():
    return pl.BlockSpec(memory_space=pltpu.SMEM)


def in_vmem():
    return pl.BlockSpec(memory_space=pltpu.VMEM)


def in_hbm():
    return pl.BlockSpec(memory_space=pltpu.HBM)


def call(kernel, scalars, arrays, outs, scratch, far_outs=(), limit=VMEM):
    shapes = [jax.ShapeDtypeStruct(shape, BF16) for shape in (*far_outs, *outs)]
    return pl.pallas_call(
        kernel,
        in_specs=[smem() for _ in scalars] + [in_vmem() for _ in arrays],
        out_specs=[in_hbm() for _ in far_outs] + [in_vmem() for _ in outs],
        out_shape=shapes,
        scratch_shapes=[
            kind(shape, dtype) if dtype is not None else kind(shape)
            for kind, shape, dtype in ((pltpu.VMEM, *s) if len(s) == 2 else s for s in scratch)
        ],
        compiler_params=pltpu.CompilerParams(vmem_limit_bytes=limit),
    )(*scalars, *arrays)


def copies(*shape):
    return (pltpu.SemaphoreType.DMA, shape, None)


def call_outward(place, counts, quadrature, fourier, folded, vertical):
    return call(
        outward,
        (place, counts, quadrature),
        (fourier, folded, vertical),
        [(TOTAL, 128), (WAVES, WAVES)],
        [((QUADS, 256, WAVES), BF16), ((TOTAL, 128), F32), ((WAVES, 128), F32), ((LOCAL, LEV * LOCAL), F32)],
    )


def call_middle(place, folded, received, table, damping):
    return call(
        middle,
        (place, folded),
        (received, damping, table),
        [],
        [
            ((TOTAL, 128), F32),
            ((SLOTS, 128, HALF), BF16),
            ((64, 128), F32),
            ((SLOTS, 64, WAVES), BF16),
            ((SLOTS, 128, HALF), F32),
            ((2 * GROUP, 512), BF16),
            ((512, 512), BF16),
            ((2 * LEV + 2, HALF, 128), F32),
            ((TOTAL, 128), BF16),
            copies(LEV),
            copies(4),
        ],
        far_outs=[(SLOTS, LOCAL, WAVES)] * LEV + [(TOTAL, 128)],
        limit=28 * 1024 * 1024,
    )


def call_homeward(place, counts, received, hot):
    shape = (ROWS, 2, LOCAL, 2, WAVES)
    (grid,) = call(
        homeward,
        (place, counts),
        (received, hot),
        [],
        [(shape, BF16), ((QUADS, TILES, 256, 128), F32), ((TOTAL, 128), F32), copies(QUADS)],
        far_outs=[shape],
    )
    return grid


def exchange(blocks):
    blocks = blocks.reshape(TOTAL // 2, 2, 128).reshape(OWN * LEV, CHUNK // 2, 2, 128)
    blocks = lax.all_to_all(blocks, AXES, split_axis=0, concat_axis=0, tiled=True, axis_index_groups=GROUPS)
    return blocks.reshape(TOTAL // 2, 2, 128).reshape(TOTAL, 128)


def on_device(fourier, quadrature, counts, folded, basis, vertical, damping):
    lev = lax.axis_index("lev").astype(jnp.int32)
    place = jnp.stack([lax.axis_index("lat").astype(jnp.int32), lev])
    fourier = fourier.transpose(0, 1, 3, 2, 4).reshape(ROWS, 64, WAVES)
    sent, hot = call_outward(place, counts, quadrature, fourier, folded, vertical)
    *pieces, sent = call_middle(place, folded, exchange(sent), basis, damping)
    parts = pieces[:1] + [
        lax.ppermute(pieces[o], "lev", [(i, (i + o) % LEV) for i in range(LEV)]) for o in range(1, LEV)
    ]
    received = exchange(sent)
    parts = jnp.stack(parts)
    parts = jnp.stack([lax.dynamic_index_in_dim(parts, (lev - x) % LEV, 0, keepdims=False) for x in range(LEV)])
    spectral = parts.reshape(2, 2, SLOTS, LOCAL, WAVES).transpose(2, 0, 3, 1, 4)
    grid = call_homeward(place, counts, received, hot)
    return spectral, grid


def solution(mesh):
    return jax.shard_map(
        on_device,
        mesh=mesh,
        in_specs=(
            P("lat", None, "lev", None, None),
            P("lat"),
            P(),
            P(),
            P("lat", None, None),
            P("lev", None),
            P(),
        ),
        out_specs=(P("lat", None, "lev", None, None), P("lat", None, "lev", None, None)),
        check_vma=False,
    )
```

```python
import jax
import jax.numpy as jnp
from jax import lax
from jax.experimental import pallas as pl
from jax.experimental.pallas import tpu as pltpu
from jax.sharding import PartitionSpec as P

F32, BF16 = jnp.float32, jnp.bfloat16
AXES = ("lat", "lev")
OWN = 64
HEMI = 32
LEV = 4
ROWS = 20
SLOTS = 10
LOCAL = 16
PART = 2 * LOCAL
WIDE = LEV * PART
TAKEN = 5
KEPT = (0, 1, 2, 3, 5, 6, 7, 8, 4, 9)
WAVES = 640
HALF = 640
QUADS = 5
GROUP = QUADS * HEMI
CHUNK = 26
STRIDE = LEV * CHUNK
TOTAL = OWN * STRIDE
VMEM = 24 * 1024 * 1024
ORDER = [d if d < HEMI else OWN - 1 + HEMI - d for d in range(OWN)]
GROUPS = [[d * LEV + x for d in ORDER for x in range(LEV)]]


def low_lanes(rows):
    return lax.broadcasted_iota(jnp.int32, (rows, 128), 1) < 64


def one_hot(folded, column, hot):
    row = folded[...].astype(F32).reshape(1, WAVES)
    for t in range(WAVES // 128):
        lanes = slice(t * 128, (t + 1) * 128)
        column[lanes, :] = jnp.broadcast_to(row[:, lanes], (128, 128)).T
    i = lax.broadcasted_iota(jnp.int32, (OWN, OWN), 0)
    d = lax.broadcasted_iota(jnp.int32, (OWN, OWN), 1)
    turn = jnp.where(d == jnp.where(i < HEMI, i, OWN - 1 + HEMI - i), 1.0, 0.0).astype(BF16)
    lanes = lax.broadcasted_iota(jnp.int32, (OWN, 128), 1)
    for k in range(SLOTS):
        waves = column[pl.ds(KEPT[k], OWN, stride=SLOTS), :].astype(jnp.int32)
        plain = jnp.concatenate(
            [jnp.where(waves == lanes + t * 128, 1.0, 0.0).astype(BF16) for t in range(WAVES // 128)], axis=1
        )
        hot[k * OWN : (k + 1) * OWN, :] = jnp.dot(turn, plain, preferred_element_type=F32).astype(BF16)


def swap_halves(low, left, right):
    return jnp.where(low, left, pltpu.roll(right, 64, 1)), jnp.where(low, pltpu.roll(left, 64, 1), right)


def outward(place, counts, quad, fourier, folded, vertical, out, hot, weighted, stage, column, couple):
    south = place[0] >= HEMI
    one_hot(folded, column, hot)
    couple[...] = vertical[...].astype(F32)
    piece = 2 * lax.rem(place[0], 8)
    line = jnp.concatenate([couple[pl.ds(piece, 1), :], couple[pl.ds(piece + 1, 1), :]], axis=1)
    stage[pl.ds(CHUNK - 1, OWN * LEV, stride=CHUNK), :] = jnp.broadcast_to(line, (OWN * LEV, 128))
    lanes = 2 * lax.broadcasted_iota(jnp.int32, (2 * PART, WAVES), 1)
    low = low_lanes(PART)
    slotted = hot[...].T

    def one_quarter(quarter):
        where = jnp.where(south, QUADS - 1 - quarter, quarter)
        for a in range(4):
            row = quarter * 4 + a
            count = counts[place[0] * ROWS + row]
            product = fourier[row].astype(F32) * quad[row]
            at = pl.multiple_of(jnp.where(south, 3 - a, a) * 2 * PART, 2 * PART)
            weighted[quarter, pl.ds(at, 2 * PART), :] = jnp.where(lanes < count, product, 0.0).astype(BF16)
        spread = jnp.dot(weighted[quarter], slotted, preferred_element_type=F32)

        def part(f, a, tile):
            return spread[(a * 2 + f) * PART : (a * 2 + f + 1) * PART, tile * 128 : (tile + 1) * 128]

        def put(x, row, values):
            stage[pl.ds(x * CHUNK + row, OWN, stride=STRIDE), :] = values

        for f in range(2):
            for half in range(2):
                for a in (0, 2):
                    blocks = [
                        block
                        for tile in (2 * half, 2 * half + 1)
                        for block in swap_halves(low, part(f, a, tile), part(f, a + 1, tile))
                    ]
                    across = jnp.concatenate(blocks, axis=0).T
                    put(2 * f + half, where * 4 + a, across[:OWN])
                    put(2 * f + half, where * 4 + a + 1, across[OWN:])
            across = jnp.concatenate([part(f, a, 4) for a in range(4)], axis=0).T
            put(2 * f, ROWS + where, across[:OWN])
            put(2 * f + 1, ROWS + where, across[OWN:])

    for quarter in range(QUADS):
        one_quarter(quarter)
    out[...] = stage[...].astype(BF16)


def middle(
    place, folded, received, damping, table,
    own, first, second, third, out, stage, turned, couple, pieces, result, rest, order, natural, ready, leave, depart,
):
    stage[...] = received[...].astype(F32)
    for x in range(LEV):
        lines = stage[pl.ds(x * CHUNK + CHUNK - 1, 8, stride=STRIDE), :]
        couple[pl.ds(x * LOCAL, 8, stride=2), :] = lines
        couple[pl.ds(x * LOCAL + 1, 8, stride=2), :] = pltpu.roll(lines, 64, 1)
    target = lax.broadcasted_iota(jnp.int32, (WIDE, 64), 0)
    level = lax.broadcasted_iota(jnp.int32, (WIDE, 64), 1)
    after = jnp.where(target >> 1 == level, 1.0, 0.0).astype(BF16)
    before = jnp.where(((target >> 5) << 4) | (target & 15) == level, 1.0, 0.0).astype(BF16)
    mixing = jnp.dot(after, couple[:, :64].astype(BF16), preferred_element_type=F32).astype(BF16)
    mixing = lax.dot_general(mixing, before, (((1,), (1,)), ((), ())), preferred_element_type=F32)
    target = lax.broadcasted_iota(jnp.int32, (WIDE, WIDE), 0)
    source = lax.broadcasted_iota(jnp.int32, (WIDE, WIDE), 1)
    mixing = jnp.where((target & 1) == ((source >> 4) & 1), mixing, 0.0).astype(BF16)
    damp = damping[...].reshape(1, WAVES)
    lanes = lax.broadcasted_iota(jnp.int32, (512, 512), 1)
    swapped = ((lanes >> 7) << 5) | (((lanes >> 5) & 3) << 7) | (lanes & 31)
    order[...] = jnp.where(lax.broadcasted_iota(jnp.int32, (512, 512), 0) == swapped, 1.0, 0.0).astype(BF16)

    def both(x, row):
        north = stage[pl.ds(x * CHUNK + row, HEMI, stride=STRIDE), :]
        south = stage[pl.ds((HEMI * LEV + x) * CHUNK + row, HEMI, stride=STRIDE), :]
        return north + south, north - south

    for quarter in range(QUADS):
        rows = slice(quarter * HEMI, (quarter + 1) * HEMI)
        for x in range(LEV):
            for side, values in enumerate(both(x, ROWS + quarter)):
                rest[side * GROUP + quarter * HEMI : side * GROUP + (quarter + 1) * HEMI, x * 128 : (x + 1) * 128] = (
                    values.astype(BF16)
                )
    placed = jnp.dot(rest[...], order[...], preferred_element_type=F32)
    for side in range(2):
        for quarter in range(QUADS):
            for a in range(4):
                natural[2 * LEV + side, pl.ds(quarter * 4 + a, HEMI, stride=ROWS), :] = placed[
                    side * GROUP + quarter * HEMI : side * GROUP + (quarter + 1) * HEMI, a * 128 : (a + 1) * 128
                ]
        turned[TAKEN - 1, side * WIDE : (side + 1) * WIDE, :] = natural[2 * LEV + side].T.astype(BF16)
    for x in range(LEV):
        for row in range(ROWS):
            for side, values in enumerate(both(x, row)):
                natural[side * LEV + x, pl.ds(row, HEMI, stride=ROWS), :] = values
        for side in range(2):
            values = natural[side * LEV + x].T
            at = side * WIDE + x * PART
            for k in range(4):
                turned[k, at : at + PART, :] = values[k * PART : (k + 1) * PART].astype(BF16)

    degrees = lax.broadcasted_iota(jnp.int32, (WIDE, WAVES), 1)
    begin = lax.rem(place[1], 2) * TAKEN
    waves = [folded[place[0] * SLOTS + begin + slot] for slot in range(TAKEN)]

    def matching(slot):
        return ((degrees ^ waves[slot]) & 1) == 0

    for slot in range(TAKEN):
        products = jnp.dot(turned[slot], table[begin + slot], preferred_element_type=F32)
        spectra = jnp.where(matching(slot), products[:WIDE], products[WIDE:])
        pieces[slot] = jnp.where(degrees >= waves[slot], spectra, 0.0).astype(BF16)
    stores = []
    for o, ref in enumerate((own, first, second, third)):
        ahead = pl.multiple_of(lax.rem(place[1] + o, LEV) * PART, PART)
        store = pltpu.make_async_copy(pieces.at[:, pl.ds(ahead, PART), :], ref, leave.at[o])
        store.start()
        stores.append(store)

    for slot in range(TAKEN):
        filtered = jnp.dot(mixing, pieces[slot], preferred_element_type=F32) * damp
        signed = jnp.where(matching(slot), filtered, -filtered)
        turned[slot] = jnp.concatenate([filtered, signed], axis=0).astype(BF16)
    for slot in range(TAKEN):
        result[slot] = lax.dot_general(
            turned[slot], table[begin + slot], (((1,), (1,)), ((), ())), preferred_element_type=F32
        )

    for side in range(2):
        natural[2 * LEV + side] = result[TAKEN - 1, side * WIDE : (side + 1) * WIDE, :].T
        for quarter in range(QUADS):
            for a in range(4):
                rest[side * GROUP + quarter * HEMI : side * GROUP + (quarter + 1) * HEMI, a * 128 : (a + 1) * 128] = (
                    natural[2 * LEV + side, pl.ds(quarter * 4 + a, HEMI, stride=ROWS), :].astype(BF16)
                )
    placed = jnp.dot(rest[...], order[...], preferred_element_type=F32)
    for side in range(2):
        for x in range(LEV):
            at = side * WIDE + x * PART
            natural[side * LEV + x] = jnp.concatenate([result[k, at : at + PART, :] for k in range(4)], axis=0).T
            start = (side * HEMI * LEV + x) * CHUNK
            for row in range(ROWS):
                stage[pl.ds(start + row, HEMI, stride=STRIDE), :] = natural[
                    side * LEV + x, pl.ds(row, HEMI, stride=ROWS), :
                ]
            for quarter in range(QUADS):
                stage[pl.ds(start + ROWS + quarter, HEMI, stride=STRIDE), :] = placed[
                    side * GROUP + quarter * HEMI : side * GROUP + (quarter + 1) * HEMI, x * 128 : (x + 1) * 128
                ]
        for part in range(2):
            rows = pl.ds((2 * side + part) * (TOTAL // 4), TOTAL // 4)
            ready[rows, :] = stage[rows, :].astype(BF16)
            store = pltpu.make_async_copy(ready.at[rows, :], out.at[rows, :], depart.at[2 * side + part])
            store.start()
            stores.append(store)
    for store in stores:
        store.wait()


def homeward(place, counts, received, hot, out, grid, slots, stage, depart):
    stores = []
    south = place[0] >= HEMI
    stage[...] = received[...].astype(F32)
    low = low_lanes(PART)
    lanes = 2 * lax.broadcasted_iota(jnp.int32, (LEV * LOCAL, WAVES), 1)

    def collect(quarter):
        where = jnp.where(south, QUADS - 1 - quarter, quarter)

        def get(x, row):
            return stage[pl.ds(x * CHUNK + row, OWN, stride=STRIDE), :]

        def put(f, a, tile, values):
            rows = slice((a * 2 + f) * PART, (a * 2 + f + 1) * PART)
            slots[quarter, rows, tile * 128 : (tile + 1) * 128] = values

        for f in range(2):
            for half in range(2):
                for a in (0, 2):
                    x = 2 * f + half
                    values = jnp.concatenate([get(x, where * 4 + a), get(x, where * 4 + a + 1)], axis=0).T
                    for tile in range(2):
                        even = values[2 * tile * PART : (2 * tile + 1) * PART]
                        odd = values[(2 * tile + 1) * PART : (2 * tile + 2) * PART]
                        left, right = swap_halves(low, even, odd)
                        put(f, a, 2 * half + tile, left)
                        put(f, a + 1, 2 * half + tile, right)
            values = jnp.concatenate([get(2 * f, ROWS + where), get(2 * f + 1, ROWS + where)], axis=0).T
            for a in range(4):
                put(f, a, 4, values[a * PART : (a + 1) * PART])

    def finish(quarter):
        values = jnp.dot(slots[quarter].astype(BF16), hot[...], preferred_element_type=F32)
        for at in range(4):
            row = quarter * 4 + jnp.where(south, 3 - at, at)
            count = counts[place[0] * ROWS + row]
            part = jnp.where(lanes < count, values[at * 64 : (at + 1) * 64], 0.0).astype(BF16)
            grid[row] = part.reshape(2, LOCAL, 2, WAVES)
        rows = pl.ds(quarter * 4, 4)
        stores.append(pltpu.make_async_copy(grid.at[rows], out.at[rows], depart.at[quarter]))
        stores[-1].start()

    for quarter in range(QUADS):
        collect(quarter)
    for quarter in range(QUADS):
        finish(quarter)
    for store in stores:
        store.wait()


def smem():
    return pl.BlockSpec(memory_space=pltpu.SMEM)


def in_vmem():
    return pl.BlockSpec(memory_space=pltpu.VMEM)


def in_hbm():
    return pl.BlockSpec(memory_space=pltpu.HBM)


def call(kernel, scalars, arrays, outs, scratch, far_outs=(), limit=VMEM):
    shapes = [jax.ShapeDtypeStruct(shape, BF16) for shape in (*far_outs, *outs)]
    return pl.pallas_call(
        kernel,
        in_specs=[smem() for _ in scalars] + [in_vmem() for _ in arrays],
        out_specs=[in_hbm() for _ in far_outs] + [in_vmem() for _ in outs],
        out_shape=shapes,
        scratch_shapes=[
            kind(shape, dtype) if dtype is not None else kind(shape)
            for kind, shape, dtype in ((pltpu.VMEM, *s) if len(s) == 2 else s for s in scratch)
        ],
        compiler_params=pltpu.CompilerParams(vmem_limit_bytes=limit),
    )(*scalars, *arrays)


def copies(*shape):
    return (pltpu.SemaphoreType.DMA, shape, None)


def call_outward(place, counts, quadrature, fourier, folded, vertical):
    return call(
        outward,
        (place, counts, quadrature),
        (fourier, folded, vertical),
        [(TOTAL, 128), (WAVES, WAVES)],
        [
            ((QUADS, 256, WAVES), BF16),
            ((TOTAL, 128), F32),
            ((WAVES, 128), F32),
            ((LOCAL, LEV * LOCAL), F32),
        ],
    )


def call_middle(place, folded, received, table, damping):
    return call(
        middle,
        (place, folded),
        (received, damping, table),
        [],
        [
            ((TOTAL, 128), F32),
            ((TAKEN, 2 * WIDE, HALF), BF16),
            ((64, 128), F32),
            ((TAKEN, WIDE, WAVES), BF16),
            ((TAKEN, 2 * WIDE, HALF), F32),
            ((2 * GROUP, 512), BF16),
            ((512, 512), BF16),
            ((2 * LEV + 2, HALF, 128), F32),
            ((TOTAL, 128), BF16),
            copies(LEV),
            copies(4),
        ],
        far_outs=[(TAKEN, PART, WAVES)] * LEV + [(TOTAL, 128)],
        limit=28 * 1024 * 1024,
    )


def call_homeward(place, counts, received, hot):
    shape = (ROWS, 2, LOCAL, 2, WAVES)
    (grid,) = call(
        homeward,
        (place, counts),
        (received, hot),
        [],
        [(shape, BF16), ((QUADS, 256, WAVES), F32), ((TOTAL, 128), F32), copies(QUADS)],
        far_outs=[shape],
    )
    return grid


def exchange(blocks):
    blocks = blocks.reshape(TOTAL // 2, 2, 128).reshape(OWN * LEV, CHUNK // 2, 2, 128)
    blocks = lax.all_to_all(blocks, AXES, split_axis=0, concat_axis=0, tiled=True, axis_index_groups=GROUPS)
    return blocks.reshape(TOTAL // 2, 2, 128).reshape(TOTAL, 128)


def on_device(fourier, quadrature, counts, folded, basis, vertical, damping):
    lev = lax.axis_index("lev").astype(jnp.int32)
    place = jnp.stack([lax.axis_index("lat").astype(jnp.int32), lev])
    fourier = fourier.transpose(0, 1, 3, 2, 4).reshape(ROWS, 2 * PART, WAVES)
    sent, hot = call_outward(place, counts, quadrature, fourier, folded, vertical)
    *pieces, sent = call_middle(place, folded, exchange(sent), basis, damping)
    parts = pieces[:1] + [
        lax.ppermute(pieces[o], "lev", [(i, (i + o) % LEV) for i in range(LEV)]) for o in range(1, LEV)
    ]
    received = exchange(sent)
    parts = jnp.stack(parts)
    parts = jnp.stack([lax.dynamic_index_in_dim(parts, (lev - x) % LEV, 0, keepdims=False) for x in range(LEV)])
    parts = parts.reshape(2, 2, TAKEN, 2, LOCAL, WAVES).transpose(1, 2, 0, 4, 3, 5)
    spectral = parts.reshape(SLOTS, 2, LOCAL, 2, WAVES)
    grid = call_homeward(place, counts, received, hot)
    return spectral, grid


def solution(mesh):
    return jax.shard_map(
        on_device,
        mesh=mesh,
        in_specs=(
            P("lat", None, "lev", None, None),
            P("lat"),
            P(),
            P(),
            P("lat", None, None),
            P("lev", None),
            P(),
        ),
        out_specs=(P("lat", None, "lev", None, None), P("lat", None, "lev", None, None)),
        check_vma=False,
    )
```

```python
import jax
import jax.numpy as jnp
from jax import lax
from jax.experimental import pallas as pl
from jax.experimental.pallas import tpu as pltpu
from jax.sharding import PartitionSpec as P

F32, BF16 = jnp.float32, jnp.bfloat16
AXES = ("lat", "lev")
OWN = 64
HEMI = 32
LEV = 4
ROWS = 20
SLOTS = 10
LOCAL = 16
PART = 2 * LOCAL
WIDE = LEV * PART
TAKEN = 5
KEPT = (0, 1, 2, 3, 5, 6, 7, 8, 4, 9)
WAVES = 640
HALF = 640
QUADS = 5
GROUP = QUADS * HEMI
CHUNK = 26
STRIDE = LEV * CHUNK
TOTAL = OWN * STRIDE
VMEM = 24 * 1024 * 1024
ORDER = [d if d < HEMI else OWN - 1 + HEMI - d for d in range(OWN)]
GROUPS = [[d * LEV + x for d in ORDER for x in range(LEV)]]


def low_lanes(rows):
    return lax.broadcasted_iota(jnp.int32, (rows, 128), 1) < 64


def one_hot(folded, column, hot):
    row = folded[...].astype(F32).reshape(1, WAVES)
    for t in range(WAVES // 128):
        lanes = slice(t * 128, (t + 1) * 128)
        column[lanes, :] = jnp.broadcast_to(row[:, lanes], (128, 128)).T
    i = lax.broadcasted_iota(jnp.int32, (OWN, OWN), 0)
    d = lax.broadcasted_iota(jnp.int32, (OWN, OWN), 1)
    turn = jnp.where(d == jnp.where(i < HEMI, i, OWN - 1 + HEMI - i), 1.0, 0.0).astype(BF16)
    lanes = lax.broadcasted_iota(jnp.int32, (OWN, 128), 1)
    for k in range(SLOTS):
        waves = column[pl.ds(KEPT[k], OWN, stride=SLOTS), :].astype(jnp.int32)
        plain = jnp.concatenate(
            [jnp.where(waves == lanes + t * 128, 1.0, 0.0).astype(BF16) for t in range(WAVES // 128)], axis=1
        )
        hot[k * OWN : (k + 1) * OWN, :] = jnp.dot(turn, plain, preferred_element_type=F32).astype(BF16)


def swap_halves(low, left, right):
    return jnp.where(low, left, pltpu.roll(right, 64, 1)), jnp.where(low, pltpu.roll(left, 64, 1), right)


def outward(place, counts, quad, fourier, folded, vertical, out, hot, weighted, stage, column, couple):
    south = place[0] >= HEMI
    one_hot(folded, column, hot)
    couple[...] = vertical[...].astype(F32)
    piece = 2 * lax.rem(place[0], 8)
    line = jnp.concatenate([couple[pl.ds(piece, 1), :], couple[pl.ds(piece + 1, 1), :]], axis=1)
    stage[pl.ds(CHUNK - 1, OWN * LEV, stride=CHUNK), :] = jnp.broadcast_to(line, (OWN * LEV, 128))
    lanes = 2 * lax.broadcasted_iota(jnp.int32, (2 * PART, WAVES), 1)
    low = low_lanes(PART)
    slotted = hot[...].T

    def one_quarter(quarter):
        where = jnp.where(south, QUADS - 1 - quarter, quarter)
        for a in range(4):
            row = quarter * 4 + a
            count = counts[place[0] * ROWS + row]
            product = fourier[row].astype(F32) * quad[row]
            at = pl.multiple_of(jnp.where(south, 3 - a, a) * 2 * PART, 2 * PART)
            weighted[quarter, pl.ds(at, 2 * PART), :] = jnp.where(lanes < count, product, 0.0).astype(BF16)
        spread = jnp.dot(weighted[quarter], slotted, preferred_element_type=F32)

        def part(f, a, tile):
            return spread[(a * 2 + f) * PART : (a * 2 + f + 1) * PART, tile * 128 : (tile + 1) * 128]

        def put(x, row, values):
            stage[pl.ds(x * CHUNK + row, OWN, stride=STRIDE), :] = values

        for f in range(2):
            for half in range(2):
                for a in (0, 2):
                    blocks = [
                        block
                        for tile in (2 * half, 2 * half + 1)
                        for block in swap_halves(low, part(f, a, tile), part(f, a + 1, tile))
                    ]
                    across = jnp.concatenate(blocks, axis=0).T
                    put(2 * f + half, where * 4 + a, across[:OWN])
                    put(2 * f + half, where * 4 + a + 1, across[OWN:])
            across = jnp.concatenate([part(f, a, 4) for a in range(4)], axis=0).T
            put(2 * f, ROWS + where, across[:OWN])
            put(2 * f + 1, ROWS + where, across[OWN:])

    for quarter in range(QUADS):
        one_quarter(quarter)
    out[...] = stage[...].astype(BF16)


def middle(
    place, folded, received, damping, table,
    own, first, second, third, out, stage, turned, couple, pieces, result, rest, order, natural, ready, leave, depart,
):
    stage[...] = received[...].astype(F32)
    for x in range(LEV):
        lines = stage[pl.ds(x * CHUNK + CHUNK - 1, 8, stride=STRIDE), :]
        couple[pl.ds(x * LOCAL, 8, stride=2), :] = lines
        couple[pl.ds(x * LOCAL + 1, 8, stride=2), :] = pltpu.roll(lines, 64, 1)
    target = lax.broadcasted_iota(jnp.int32, (WIDE, 64), 0)
    level = lax.broadcasted_iota(jnp.int32, (WIDE, 64), 1)
    after = jnp.where(target >> 1 == level, 1.0, 0.0).astype(BF16)
    before = jnp.where(((target >> 5) << 4) | (target & 15) == level, 1.0, 0.0).astype(BF16)
    mixing = jnp.dot(after, couple[:, :64].astype(BF16), preferred_element_type=F32).astype(BF16)
    mixing = lax.dot_general(mixing, before, (((1,), (1,)), ((), ())), preferred_element_type=F32)
    target = lax.broadcasted_iota(jnp.int32, (WIDE, WIDE), 0)
    source = lax.broadcasted_iota(jnp.int32, (WIDE, WIDE), 1)
    mixing = jnp.where((target & 1) == ((source >> 4) & 1), mixing, 0.0).astype(BF16)
    damp = damping[...].reshape(1, WAVES)
    lanes = lax.broadcasted_iota(jnp.int32, (512, 512), 1)
    swapped = ((lanes >> 7) << 5) | (((lanes >> 5) & 3) << 7) | (lanes & 31)
    order[...] = jnp.where(lax.broadcasted_iota(jnp.int32, (512, 512), 0) == swapped, 1.0, 0.0).astype(BF16)

    def both(x, row):
        north = stage[pl.ds(x * CHUNK + row, HEMI, stride=STRIDE), :]
        south = stage[pl.ds((HEMI * LEV + x) * CHUNK + row, HEMI, stride=STRIDE), :]
        return north + south, north - south

    for quarter in range(QUADS):
        rows = slice(quarter * HEMI, (quarter + 1) * HEMI)
        for x in range(LEV):
            for side, values in enumerate(both(x, ROWS + quarter)):
                rest[side * GROUP + quarter * HEMI : side * GROUP + (quarter + 1) * HEMI, x * 128 : (x + 1) * 128] = (
                    values.astype(BF16)
                )
    placed = jnp.dot(rest[...], order[...], preferred_element_type=F32)
    for side in range(2):
        for quarter in range(QUADS):
            for a in range(4):
                natural[2 * LEV + side, pl.ds(quarter * 4 + a, HEMI, stride=ROWS), :] = placed[
                    side * GROUP + quarter * HEMI : side * GROUP + (quarter + 1) * HEMI, a * 128 : (a + 1) * 128
                ]
        turned[TAKEN - 1, side * WIDE : (side + 1) * WIDE, :] = natural[2 * LEV + side].T.astype(BF16)
    for x in range(LEV):
        for row in range(ROWS):
            for side, values in enumerate(both(x, row)):
                natural[side * LEV + x, pl.ds(row, HEMI, stride=ROWS), :] = values
        for side in range(2):
            values = natural[side * LEV + x].T
            at = side * WIDE + x * PART
            for k in range(4):
                turned[k, at : at + PART, :] = values[k * PART : (k + 1) * PART].astype(BF16)

    degrees = lax.broadcasted_iota(jnp.int32, (WIDE, WAVES), 1)
    begin = lax.rem(place[1], 2) * TAKEN
    waves = [folded[place[0] * SLOTS + begin + slot] for slot in range(TAKEN)]

    def matching(slot):
        return ((degrees ^ waves[slot]) & 1) == 0

    for slot in range(TAKEN):
        products = jnp.dot(turned[slot], table[begin + slot], preferred_element_type=F32)
        spectra = jnp.where(matching(slot), products[:WIDE], products[WIDE:])
        pieces[slot] = jnp.where(degrees >= waves[slot], spectra, 0.0).astype(BF16)
    for slot in range(TAKEN):
        filtered = jnp.dot(mixing, pieces[slot], preferred_element_type=F32) * damp
        signed = jnp.where(matching(slot), filtered, -filtered)
        turned[slot] = jnp.concatenate([filtered, signed], axis=0).astype(BF16)
    for slot in range(TAKEN):
        result[slot] = lax.dot_general(
            turned[slot], table[begin + slot], (((1,), (1,)), ((), ())), preferred_element_type=F32
        )

    stores = []
    for o, ref in enumerate((own, first, second, third)):
        ahead = pl.multiple_of(lax.rem(place[1] + o, LEV) * PART, PART)
        store = pltpu.make_async_copy(pieces.at[:, pl.ds(ahead, PART), :], ref, leave.at[o])
        store.start()
        stores.append(store)

    for side in range(2):
        natural[2 * LEV + side] = result[TAKEN - 1, side * WIDE : (side + 1) * WIDE, :].T
        for quarter in range(QUADS):
            for a in range(4):
                rest[side * GROUP + quarter * HEMI : side * GROUP + (quarter + 1) * HEMI, a * 128 : (a + 1) * 128] = (
                    natural[2 * LEV + side, pl.ds(quarter * 4 + a, HEMI, stride=ROWS), :].astype(BF16)
                )
    placed = jnp.dot(rest[...], order[...], preferred_element_type=F32)
    for side in range(2):
        for x in range(LEV):
            at = side * WIDE + x * PART
            natural[side * LEV + x] = jnp.concatenate([result[k, at : at + PART, :] for k in range(4)], axis=0).T
            start = (side * HEMI * LEV + x) * CHUNK
            for row in range(ROWS):
                stage[pl.ds(start + row, HEMI, stride=STRIDE), :] = natural[
                    side * LEV + x, pl.ds(row, HEMI, stride=ROWS), :
                ]
            for quarter in range(QUADS):
                stage[pl.ds(start + ROWS + quarter, HEMI, stride=STRIDE), :] = placed[
                    side * GROUP + quarter * HEMI : side * GROUP + (quarter + 1) * HEMI, x * 128 : (x + 1) * 128
                ]
        for part in range(2):
            rows = pl.ds((2 * side + part) * (TOTAL // 4), TOTAL // 4)
            ready[rows, :] = stage[rows, :].astype(BF16)
            store = pltpu.make_async_copy(ready.at[rows, :], out.at[rows, :], depart.at[2 * side + part])
            store.start()
            stores.append(store)
    for store in stores:
        store.wait()


def homeward(place, counts, received, hot, out, grid, slots, stage, depart):
    stores = []
    south = place[0] >= HEMI
    stage[...] = received[...].astype(F32)
    low = low_lanes(PART)
    lanes = 2 * lax.broadcasted_iota(jnp.int32, (LEV * LOCAL, WAVES), 1)

    def collect(quarter):
        where = jnp.where(south, QUADS - 1 - quarter, quarter)

        def get(x, row):
            return stage[pl.ds(x * CHUNK + row, OWN, stride=STRIDE), :]

        def put(f, a, tile, values):
            rows = slice((a * 2 + f) * PART, (a * 2 + f + 1) * PART)
            slots[quarter, rows, tile * 128 : (tile + 1) * 128] = values

        for f in range(2):
            for half in range(2):
                for a in (0, 2):
                    x = 2 * f + half
                    values = jnp.concatenate([get(x, where * 4 + a), get(x, where * 4 + a + 1)], axis=0).T
                    for tile in range(2):
                        even = values[2 * tile * PART : (2 * tile + 1) * PART]
                        odd = values[(2 * tile + 1) * PART : (2 * tile + 2) * PART]
                        left, right = swap_halves(low, even, odd)
                        put(f, a, 2 * half + tile, left)
                        put(f, a + 1, 2 * half + tile, right)
            values = jnp.concatenate([get(2 * f, ROWS + where), get(2 * f + 1, ROWS + where)], axis=0).T
            for a in range(4):
                put(f, a, 4, values[a * PART : (a + 1) * PART])

    def finish(quarter):
        values = jnp.dot(slots[quarter].astype(BF16), hot[...], preferred_element_type=F32)
        for at in range(4):
            row = quarter * 4 + jnp.where(south, 3 - at, at)
            count = counts[place[0] * ROWS + row]
            part = jnp.where(lanes < count, values[at * 64 : (at + 1) * 64], 0.0).astype(BF16)
            grid[row] = part.reshape(2, LOCAL, 2, WAVES)
        rows = pl.ds(quarter * 4, 4)
        stores.append(pltpu.make_async_copy(grid.at[rows], out.at[rows], depart.at[quarter]))
        stores[-1].start()

    for quarter in range(QUADS):
        collect(quarter)
    for quarter in range(QUADS):
        finish(quarter)
    for store in stores:
        store.wait()


def smem():
    return pl.BlockSpec(memory_space=pltpu.SMEM)


def in_vmem():
    return pl.BlockSpec(memory_space=pltpu.VMEM)


def in_hbm():
    return pl.BlockSpec(memory_space=pltpu.HBM)


def call(kernel, scalars, arrays, outs, scratch, far_outs=(), limit=VMEM):
    shapes = [jax.ShapeDtypeStruct(shape, BF16) for shape in (*far_outs, *outs)]
    return pl.pallas_call(
        kernel,
        in_specs=[smem() for _ in scalars] + [in_vmem() for _ in arrays],
        out_specs=[in_hbm() for _ in far_outs] + [in_vmem() for _ in outs],
        out_shape=shapes,
        scratch_shapes=[
            kind(shape, dtype) if dtype is not None else kind(shape)
            for kind, shape, dtype in ((pltpu.VMEM, *s) if len(s) == 2 else s for s in scratch)
        ],
        compiler_params=pltpu.CompilerParams(vmem_limit_bytes=limit),
    )(*scalars, *arrays)


def copies(*shape):
    return (pltpu.SemaphoreType.DMA, shape, None)


def call_outward(place, counts, quadrature, fourier, folded, vertical):
    return call(
        outward,
        (place, counts, quadrature),
        (fourier, folded, vertical),
        [(TOTAL, 128), (WAVES, WAVES)],
        [
            ((QUADS, 256, WAVES), BF16),
            ((TOTAL, 128), F32),
            ((WAVES, 128), F32),
            ((LOCAL, LEV * LOCAL), F32),
        ],
    )


def call_middle(place, folded, received, table, damping):
    return call(
        middle,
        (place, folded),
        (received, damping, table),
        [],
        [
            ((TOTAL, 128), F32),
            ((TAKEN, 2 * WIDE, HALF), BF16),
            ((64, 128), F32),
            ((TAKEN, WIDE, WAVES), BF16),
            ((TAKEN, 2 * WIDE, HALF), F32),
            ((2 * GROUP, 512), BF16),
            ((512, 512), BF16),
            ((2 * LEV + 2, HALF, 128), F32),
            ((TOTAL, 128), BF16),
            copies(LEV),
            copies(4),
        ],
        far_outs=[(TAKEN, PART, WAVES)] * LEV + [(TOTAL, 128)],
        limit=28 * 1024 * 1024,
    )


def call_homeward(place, counts, received, hot):
    shape = (ROWS, 2, LOCAL, 2, WAVES)
    (grid,) = call(
        homeward,
        (place, counts),
        (received, hot),
        [],
        [(shape, BF16), ((QUADS, 256, WAVES), F32), ((TOTAL, 128), F32), copies(QUADS)],
        far_outs=[shape],
    )
    return grid


def exchange(blocks):
    blocks = blocks.reshape(TOTAL // 2, 2, 128).reshape(OWN * LEV, CHUNK // 2, 2, 128)
    blocks = lax.all_to_all(blocks, AXES, split_axis=0, concat_axis=0, tiled=True, axis_index_groups=GROUPS)
    return blocks.reshape(TOTAL // 2, 2, 128).reshape(TOTAL, 128)


def on_device(fourier, quadrature, counts, folded, basis, vertical, damping):
    lev = lax.axis_index("lev").astype(jnp.int32)
    place = jnp.stack([lax.axis_index("lat").astype(jnp.int32), lev])
    fourier = fourier.transpose(0, 1, 3, 2, 4).reshape(ROWS, 2 * PART, WAVES)
    sent, hot = call_outward(place, counts, quadrature, fourier, folded, vertical)
    *pieces, sent = call_middle(place, folded, exchange(sent), basis, damping)
    parts = pieces[:1] + [
        lax.ppermute(pieces[o], "lev", [(i, (i + o) % LEV) for i in range(LEV)]) for o in range(1, LEV)
    ]
    received = exchange(sent)
    parts = jnp.stack(parts)
    parts = jnp.stack([lax.dynamic_index_in_dim(parts, (lev - x) % LEV, 0, keepdims=False) for x in range(LEV)])
    parts = parts.reshape(2, 2, TAKEN, 2, LOCAL, WAVES).transpose(1, 2, 0, 4, 3, 5)
    spectral = parts.reshape(SLOTS, 2, LOCAL, 2, WAVES)
    grid = call_homeward(place, counts, received, hot)
    return spectral, grid


def solution(mesh):
    return jax.shard_map(
        on_device,
        mesh=mesh,
        in_specs=(
            P("lat", None, "lev", None, None),
            P("lat"),
            P(),
            P(),
            P("lat", None, None),
            P("lev", None),
            P(),
        ),
        out_specs=(P("lat", None, "lev", None, None), P("lat", None, "lev", None, None)),
        check_vma=False,
    )
```
